256 devices in a mesh: section: 8 (over x_lo, y), expert: 32 (over z, x_hi, core).
Axes of the slice: x: 4 (x_hi: 2, x_lo: 2; x = x_hi * 2 + x_lo), y: 4, z: 8, core: 2. Of those that a mesh axis runs over, the one named last changes fastest.
Arguments:
- queries: bfloat16 [8192, 64, 576], P('expert', 'section'), may hold values from -64 to 64
- group_latent: bfloat16 [8192, 576], P('expert'), may hold values from -6 to 6
- cache_latent: bfloat16 [128, 32, 576], P('expert'), may hold values from -6 to 6
- unit_ids: int32 [16], replicated, may hold values from 0 to 127, as said below
- tokens_b: bfloat16 [1024, 7168], P('expert'), may hold values from -6 to 6
- expert_ids: int32 [1024, 8], P('expert'), may hold values from 0 to 31, all different within a row; in each aligned block of 32 rows (0 to 31, 32 to 63, ...) at most 10 rows name the same one
- affinity: float32 [1024, 8], P('expert'), may hold values from 0.05 to 1
- gate_w: bfloat16 [32, 7168, 1024], P('expert', None, 'section'), may hold values from -0.0625 to 0.0625
- up_w: bfloat16 [32, 7168, 1024], P('expert', None, 'section'), may hold values from -0.0625 to 0.0625
- down_w: bfloat16 [32, 1024, 7168], P('expert', 'section'), may hold values from -0.1875 to 0.1875
Outputs:
- context: bfloat16 [8192, 64, 512], P('expert', 'section')
- moe_out: bfloat16 [1024, 7168], P('expert')
The draws below stay inside these ranges and needn't reach their ends.
Inputs may be any that keep to these rules, and one draw needn't show every extreme that they name: `expert_ids`: each row names 8 different experts; among the rows of one index of expert no expert is named more than 10 times, a bound that some block reaches. `unit_ids`: distinct unit numbers; unit u is held by index u // 4 of expert. The selected units are spread as evenly as possible over the indices of expert: none holds more than 1 of them, and some index exactly 1.
All inputs are finite; a program needn't handle non-finite values.
Results may differ from the reference program's by a relative error of at most 0.012.
Values may be sent and summed in bfloat16 or wider, within the bound.
No kernel may reach another device: no remote copies, remote signals or barrier semaphores. Data moves between devices by JAX's collectives and lax.ppermute only.
A program may use at most 128 MiB of HBM per device.

```python
import math
import jax
import jax.numpy as jnp
import numpy as np
from jax import lax

D = 7168
FF = 1024
HEADS = 64
QK = 576
LATENT = 512
TOP = 8
ULEN = 32
SEL = 16
U_DEV = 4
TOKA_DEV = 256
TOKB_DEV = 32
EXPERTS = 32
CAP = 10
FF_DEV = 128
TOKA = 8192
WIN = 256
TOKB = 1024
UNITS = 128
N_SECTION = 8
N_EXPERT = 32


def latent_draw_of(key):
    return jnp.clip(jax.random.normal(jax.random.fold_in(key, 101), (TOKA, QK), jnp.float32), -6.0, 6.0)


def draw_group_latent(key, part):
    latent_draw = latent_draw_of(key)
    return latent_draw.astype(jnp.bfloat16)


def draw_queries(key, part):
    key = jax.random.fold_in(key, 2)
    query_draw = jnp.clip(jax.random.normal(key, (TOKA, HEADS, QK), jnp.float32), -6.0, 6.0)
    return query_draw.astype(jnp.bfloat16)


def draw_unit_ids(key, part):
    key = jax.random.fold_in(key, 4)
    n_owner = UNITS // U_DEV
    owners = jax.random.permutation(jax.random.fold_in(key, 1), n_owner)
    slot_number = jnp.arange(SEL, dtype=jnp.int32)
    owner_of = owners[slot_number % n_owner]
    first_unit = jax.random.randint(jax.random.fold_in(key, 2), (n_owner,), 0, U_DEV)
    local_unit = (first_unit[owner_of] + slot_number // n_owner) % U_DEV
    return (owner_of * U_DEV + local_unit).astype(jnp.int32)


def steps_of(rng, dims, shards, smallest, top_value):
    def one(dim, blocks):
        draws = jax.random.uniform(jax.random.fold_in(jax.random.fold_in(rng, 6), dim), (blocks,), jnp.float32, smallest / len(shards), top_value / len(shards))
        return jnp.repeat(jnp.exp(draws), dims[dim] // blocks).reshape((-1,) + (1,) * (len(dims) - dim - 1))

    loudness = one(*shards[0])
    for cut in shards[1:]:
        loudness = loudness * one(*cut)
    return loudness


def routed_block(rng, own, number, rows, count, top, reach, skew):
    sequence = jax.random.permutation(rng, count)
    packed, usual = load_shares(count, rows * top, reach, skew, True), load_shares(count, rows * top, reach, skew, False)
    places = jnp.arange(count)

    def named(sizes, offset_by):
        used = int((sizes > 0).sum())
        fixed = max(1, used // 4)
        shifted = fixed + (places - fixed + offset_by * (used - fixed)) % max(1, count - fixed)
        return jnp.zeros((count,), jnp.int32).at[sequence[jnp.where(places < fixed, places, shifted)]].set(jnp.asarray(sizes, jnp.int32))

    sizes = jnp.where(number % 4 == 0, named(packed, number // 4), named(usual, number - number // 4 - 1))
    mixed = jax.random.permutation(jax.random.fold_in(own, 3), count)
    giver, sink = mixed[0:count // 2 * 2:2], mixed[1:count // 2 * 2:2]
    margin = jnp.minimum(sizes[giver] - 1, reach - sizes[sink]) // 2
    margin = jnp.where((giver == sequence[0]) | (sink == sequence[0]) | (sizes[sink] == 0), 0, jnp.maximum(margin, 0))
    shifted = jax.random.randint(jax.random.fold_in(own, 4), (count // 2,), 0, 1 << 20) % (margin + 1)
    sizes = sizes.at[giver].add(-shifted).at[sink].add(shifted)
    items = jnp.searchsorted(jnp.cumsum(sizes), jnp.arange(rows * top), side="right").astype(jnp.int32)
    grid = items.reshape(top, rows).T
    grid = grid[jax.random.permutation(jax.random.fold_in(own, 1), rows)]
    offset_by = jax.random.randint(jax.random.fold_in(own, 2), (rows, 1), 0, top)
    return jnp.take_along_axis(grid, (jnp.arange(top)[None, :] + offset_by) % top, axis=1)


def load_shares(count, total, most, skew, full):
    weights = [(1 << 20) // math.isqrt(standing ** skew) + 1 for standing in range(1, count + 1)]
    largest = most if full else min(most, max(-(-total // count), total * weights[0] // sum(weights)))
    least = 1 if total - largest >= count - 1 else 0
    given, spare = [largest] + [least] * (count - 1), total - largest - least * (count - 1)
    while spare > 0:
        movable = [i for i in range(1, count) if given[i] < largest] or [i for i in range(1, count) if given[i] < most]
        mass, remaining = sum([weights[i] for i in movable]), spare
        for i in movable:
            addition = min(most - given[i], max(1, remaining * weights[i] // mass), spare)
            given[i] = given[i] + addition
            spare = spare - addition
    return np.array(given)


def bell_draw(key, shape, width, bound, shards=(), kind=jnp.bfloat16):
    loudness = steps_of(key, shape, shards, -0.22, 0.18) if shards else 1.0
    array = jax.random.normal(key, shape, jnp.float32) * width * loudness
    return jnp.minimum(jnp.maximum(array, -bound), bound).astype(kind)


def setup_inputs(seed: int = 0) -> dict:
    key_of = jax.random.split(jax.random.key(seed), 11)
    queries = draw_queries(jax.random.fold_in(key_of[10], 71), 0)
    group_latent = draw_group_latent(jax.random.fold_in(key_of[10], 71), 0)
    cache_latent = bell_draw(key_of[2], (UNITS, ULEN, QK), 1.0, 6.0, ((0, 32),))
    unit_ids = draw_unit_ids(jax.random.fold_in(key_of[10], 71), 0)
    tokens_b = bell_draw(key_of[4], (TOKB, D), 1.0, 6.0, ((0, 32),))
    expert_ids_keys = jax.random.split(jax.random.fold_in(key_of[5], 1), TOKB // TOKB_DEV)
    expert_ids_turns = jax.random.permutation(jax.random.fold_in(key_of[5], 3), TOKB // TOKB_DEV)
    expert_ids = jax.vmap(lambda own, number: routed_block(jax.random.fold_in(key_of[5], 2), own, number, TOKB_DEV, EXPERTS, TOP, CAP, 1))(expert_ids_keys, expert_ids_turns).reshape((TOKB, TOP))
    affinity = jnp.clip(jnp.exp(math.log(1.0) - 2.9957323 * jax.random.uniform(key_of[6], (TOKB, TOP), jnp.float32) ** steps_of(key_of[6], (TOKB, TOP), ((0, 32),), -0.2, 0.2)), 0.05, 1.0)
    gate_w = bell_draw(key_of[7], (EXPERTS, D, FF), D ** -0.5, 0.0625, ((0, 32), (2, 8)))
    up_w = bell_draw(key_of[8], (EXPERTS, D, FF), D ** -0.5, 0.0625, ((0, 32), (2, 8)))
    down_w = bell_draw(key_of[9], (EXPERTS, FF, D), FF ** -0.5, 0.1875, ((0, 32), (1, 8)))
    return {"queries": queries, "group_latent": group_latent, "cache_latent": cache_latent, "unit_ids": unit_ids, "tokens_b": tokens_b, "expert_ids": expert_ids, "affinity": affinity, "gate_w": gate_w, "up_w": up_w, "down_w": down_w}


score_scale = 192.0 ** -0.5
route_scale = 2.5


def reference(queries, group_latent, cache_latent, unit_ids, tokens_b, expert_ids, affinity, gate_w, up_w, down_w):
    unit_rows = cache_latent[unit_ids].reshape(SEL * ULEN, QK).astype(jnp.float32)
    padded_keys = jnp.concatenate([jnp.zeros((TOKA_DEV, QK), jnp.bfloat16), group_latent], 0)

    def attend_block(block_index):
        query_block = lax.dynamic_slice_in_dim(queries, block_index * TOKA_DEV, TOKA_DEV, 0).astype(jnp.float32)
        key_rows = lax.dynamic_slice_in_dim(padded_keys, block_index * TOKA_DEV, 2 * TOKA_DEV, 0).astype(jnp.float32)
        query_pos = block_index * TOKA_DEV + jnp.arange(TOKA_DEV, dtype=jnp.int32)[:, None]
        key_pos = block_index * TOKA_DEV - TOKA_DEV + jnp.arange(2 * TOKA_DEV, dtype=jnp.int32)[None, :]
        allowed = ((key_pos <= query_pos) & (key_pos > query_pos - WIN) & (key_pos >= 0))[:, None, :]
        win_s = jnp.einsum("thc,kc->thk", query_block, key_rows) * score_scale
        unit_s = jnp.einsum("thc,kc->thk", query_block, unit_rows) * score_scale
        top_s = jnp.maximum(jnp.max(jnp.where(allowed, win_s, -1e30), -1), jnp.max(unit_s, -1))[..., None]
        win_p = jnp.where(allowed, jnp.exp(win_s - top_s), 0.0)
        unit_p = jnp.exp(unit_s - top_s)
        denominator = jnp.sum(win_p, -1) + jnp.sum(unit_p, -1)
        win_r = lax.optimization_barrier(win_p.astype(jnp.bfloat16)).astype(jnp.float32)
        unit_r = lax.optimization_barrier(unit_p.astype(jnp.bfloat16)).astype(jnp.float32)
        numerator = jnp.einsum("thk,kc->thc", win_r, key_rows[:, :LATENT])
        numerator = numerator + jnp.einsum("thk,kc->thc", unit_r, unit_rows[:, :LATENT])
        return (numerator / denominator[..., None]).astype(jnp.bfloat16)

    context = lax.map(attend_block, jnp.arange(N_EXPERT, dtype=jnp.int32)).reshape(TOKA, HEADS, LATENT)

    flat_blocks = expert_ids.reshape(N_EXPERT, TOKB_DEV * TOP)
    onehot = (flat_blocks[:, :, None] == jnp.arange(EXPERTS, dtype=jnp.int32)[None, None, :]).astype(jnp.int32)
    slot_rank = jnp.sum((jnp.cumsum(onehot, 1) - 1) * onehot, 2)
    source = jnp.arange(N_EXPERT, dtype=jnp.int32)[:, None]
    slot_place = (source * CAP + slot_rank).reshape(-1).astype(jnp.int32)
    token_of = (jnp.arange(TOKB * TOP, dtype=jnp.int32) // TOP).astype(jnp.int32)
    flat_experts = expert_ids.reshape(-1)
    slot_table = jnp.full((EXPERTS, N_EXPERT * CAP), TOKB, jnp.int32).at[flat_experts, slot_place].set(token_of)
    route_share = route_scale * affinity / jnp.sum(affinity, 1, keepdims=True)
    weight_table = jnp.zeros((EXPERTS, N_EXPERT * CAP), jnp.float32).at[flat_experts, slot_place].set(route_share.reshape(-1))
    padded_rows = jnp.concatenate([tokens_b, jnp.zeros((1, D), jnp.bfloat16)], 0)

    def one_expert(running, inputs):
        rows_index, weights, gate_rows, up_rows, down_rows = inputs
        flat_rows = padded_rows[rows_index]
        gate_part = jnp.dot(flat_rows, gate_rows, preferred_element_type=jnp.float32)
        up_part = jnp.dot(flat_rows, up_rows, preferred_element_type=jnp.float32)
        hidden = (jax.nn.silu(gate_part) * up_part).astype(jnp.bfloat16)
        summed = jnp.zeros((N_EXPERT * CAP, D), jnp.float32)
        for section_block in range(N_SECTION):
            start_unit = section_block * FF_DEV
            block_out = jnp.dot(hidden[:, start_unit:start_unit + FF_DEV], down_rows[start_unit:start_unit + FF_DEV], preferred_element_type=jnp.float32)
            summed = summed + lax.optimization_barrier(block_out.astype(jnp.bfloat16)).astype(jnp.float32)
        return running.at[rows_index].add(weights[:, None] * summed), None

    running, _ = lax.scan(one_expert, jnp.zeros((TOKB + 1, D), jnp.float32), (slot_table, weight_table, gate_w, up_w, down_w))
    moe_out = running[:TOKB].astype(jnp.bfloat16)
    return (context, moe_out)
```

```python
import jax
import jax.numpy as jnp
from jax import lax
from jax.sharding import PartitionSpec as P

LATENT = 512
N_EXPERT = 32
N_SECTION = 8
N_Y = 4
CAP = 10
LANES = 128

score_scale = 192.0 ** (-0.5)
route_scale = 2.5


def along_y(value, step):
    pairs = [
        (a * N_Y + y, a * N_Y + (y + step) % N_Y) for a in range(2) for y in range(N_Y)
    ]
    return lax.ppermute(value, "section", pairs)


def across_x(value):
    pairs = [(s, (s + N_Y) % N_SECTION) for s in range(N_SECTION)]
    return lax.ppermute(value, "section", pairs)


def spread(value):
    copies = jnp.broadcast_to(value[None], (N_SECTION,) + value.shape)
    return lax.all_to_all(copies, "section", split_axis=0, concat_axis=0, tiled=True)


def attend(queries, previous, group_latent, unit_rows):
    count = queries.shape[0]
    own_index = lax.axis_index("expert")
    key_rows = jnp.concatenate([previous, group_latent], 0)
    query_pos = own_index * count + jnp.arange(count, dtype=jnp.int32)[:, None]
    key_pos = own_index * count - count + jnp.arange(2 * count, dtype=jnp.int32)[None, :]
    allowed = ((key_pos <= query_pos) & (key_pos > query_pos - count) & (key_pos >= 0))[:, None, :]
    win_s = (
        jnp.einsum("thc,kc->thk", queries, key_rows, preferred_element_type=jnp.float32)
        * score_scale
    )
    unit_s = (
        jnp.einsum("thc,kc->thk", queries, unit_rows, preferred_element_type=jnp.float32)
        * score_scale
    )
    top_s = jnp.maximum(
        jnp.max(jnp.where(allowed, win_s, -1e30), -1), jnp.max(unit_s, -1)
    )[..., None]
    win_p = jnp.where(allowed, jnp.exp(win_s - top_s), 0.0)
    unit_p = jnp.exp(unit_s - top_s)
    denominator = jnp.sum(win_p, -1) + jnp.sum(unit_p, -1)
    numerator = jnp.einsum(
        "thk,kc->thc",
        win_p.astype(jnp.bfloat16),
        key_rows[:, :LATENT],
        preferred_element_type=jnp.float32,
    )
    numerator = numerator + jnp.einsum(
        "thk,kc->thc",
        unit_p.astype(jnp.bfloat16),
        unit_rows[:, :LATENT],
        preferred_element_type=jnp.float32,
    )
    return (numerator / denominator[..., None]).astype(jnp.bfloat16)


def per_device(
    queries,
    group_latent,
    cache_latent,
    unit_ids,
    tokens_b,
    expert_ids,
    affinity,
    gate_w,
    up_w,
    down_w,
):
    own_s = lax.axis_index("section")
    own_e = lax.axis_index("expert")
    own_x, own_y = own_s // N_Y, own_s % N_Y
    tok_count, width = tokens_b.shape
    part = width // N_SECTION
    chunks = part // LANES
    half = width // 2
    f_dev = gate_w.shape[2]

    gate_all, up_all = gate_w[0], up_w[0]
    gate_up = jnp.concatenate([gate_all, up_all], 1)
    other_half = across_x(lax.dynamic_slice_in_dim(gate_up, (1 - own_x) * half, half, 0))
    own_half = lax.dynamic_slice_in_dim(gate_up, own_x * half, half, 0)
    down_cut = down_w[0].reshape(f_dev, N_SECTION, part).transpose(1, 0, 2)
    down_all = lax.all_to_all(down_cut, "section", split_axis=0, concat_axis=0, tiled=True)
    down_all = down_all.reshape(N_SECTION * f_dev, part)

    previous = lax.ppermute(
        group_latent, "expert", [(i, i + 1) for i in range(N_EXPERT - 1)]
    )

    experts = jnp.arange(N_EXPERT, dtype=jnp.int32)
    named = jnp.any(expert_ids[:, :, None] == experts[None, None, :], 1)
    rank = jnp.cumsum(named.astype(jnp.int32), 0) - 1
    slot = jnp.where(named, rank, -CAP * chunks)
    place = jnp.arange(chunks, dtype=jnp.int32)[:, None] * CAP + slot.T[:, None, :]
    place = jnp.where(slot.T[:, None, :] < 0, -1, place).reshape(N_EXPERT, chunks * tok_count)
    rows = -(-CAP * chunks // 8) * 8
    picks = (place[:, None, :] == jnp.arange(rows, dtype=jnp.int32)[None, :, None])
    tok_part = lax.dynamic_slice_in_dim(tokens_b, own_s * part, part, 1)
    tok_stack = tok_part.reshape(tok_count, chunks, LANES).transpose(1, 0, 2)
    tok_stack = tok_stack.reshape(chunks * tok_count, LANES)
    outgoing = jnp.einsum(
        "eqk,kd->eqd",
        picks.astype(jnp.bfloat16),
        tok_stack,
        preferred_element_type=jnp.float32,
    ).astype(jnp.bfloat16)

    held = cache_latent.shape[0]
    mine = jnp.sum(jnp.where(unit_ids // held == own_e, unit_ids % held, 0))
    unit_len, qk = cache_latent.shape[1:]
    cut = unit_len // N_SECTION
    unit_cut = lax.dynamic_slice(cache_latent, (mine, own_s * cut, 0), (1, cut, qk))
    unit_cut = unit_cut.reshape(1, cut * qk // LANES, LANES)
    unit_cut = jnp.broadcast_to(unit_cut, (N_EXPERT,) + unit_cut.shape[1:])

    sent = jnp.concatenate([outgoing[:, : CAP * chunks], unit_cut], 1)
    got = lax.all_to_all(sent, "expert", split_axis=0, concat_axis=0, tiled=True)

    units = got[:, CAP * chunks :][unit_ids // held]
    units = spread(units.reshape(-1, LANES))
    unit_rows = units.reshape(-1, qk)

    x_own = got[:, : CAP * chunks].reshape(N_EXPERT, chunks, CAP, LANES).transpose(2, 0, 1, 3)
    x_own = x_own.reshape(CAP * N_EXPERT, part)
    n_rows = CAP * N_EXPERT
    first, second = x_own[: n_rows // 2], x_own[n_rows // 2 :]
    before_1 = along_y(first, 1)
    after_2 = along_y(second, -1)
    before_2 = along_y(second, 1)
    after_1 = along_y(first, -1)
    far_1 = along_y(before_1, 1)
    far_2 = along_y(after_2, -1)
    x_half = jnp.stack(
        [
            x_own,
            jnp.concatenate([before_1, before_2], 0),
            jnp.concatenate([after_1, after_2], 0),
            jnp.concatenate([far_1, far_2], 0),
        ],
        0,
    )
    order = (own_y + jnp.array([0, 3, 1, 2], jnp.int32)) % N_Y
    w_half = jnp.concatenate([own_half, other_half], 1).reshape(N_Y, part, 4 * f_dev)[order]
    sums = jnp.einsum("ymk,ykf->mf", x_half, w_half, preferred_element_type=jnp.float32)
    from_x = across_x(sums[:, 2 * f_dev :].astype(jnp.bfloat16))
    both = sums[:, : 2 * f_dev] + from_x.astype(jnp.float32)
    hidden = (jax.nn.silu(both[:, :f_dev]) * both[:, f_dev:]).astype(jnp.bfloat16)
    hidden_all = spread(hidden)

    expert_out = jnp.einsum(
        "smf,sfd->md",
        hidden_all,
        down_all.reshape(N_SECTION, f_dev, part),
        preferred_element_type=jnp.float32,
    ).astype(jnp.bfloat16)
    back = expert_out.reshape(CAP, N_EXPERT, chunks, LANES).transpose(1, 2, 0, 3)
    back = back.reshape(N_EXPERT, CAP * chunks, LANES)
    back = jnp.pad(back, ((0, 0), (0, rows - CAP * chunks), (0, 0)))
    returned = lax.all_to_all(back, "expert", split_axis=0, concat_axis=0, tiled=True)

    route_share = route_scale * affinity / jnp.sum(affinity, 1, keepdims=True)
    share_e = jnp.sum(
        jnp.where(expert_ids[:, :, None] == experts[None, None, :], route_share[:, :, None], 0.0), 1
    )
    high = share_e.astype(jnp.bfloat16)
    low = (share_e - high.astype(jnp.float32)).astype(jnp.bfloat16)
    at = place.reshape(N_EXPERT, chunks, tok_count).transpose(1, 2, 0)
    hit = at[..., None] == jnp.arange(rows, dtype=jnp.int32)
    total = jnp.zeros((chunks, tok_count, LANES), jnp.float32)
    for weight in (high, low):
        mix = jnp.where(hit, weight[None, :, :, None], jnp.bfloat16(0))
        total = total + jnp.einsum(
            "jteq,eqd->jtd", mix, returned, preferred_element_type=jnp.float32
        )
    out_part = total.astype(jnp.bfloat16).transpose(1, 0, 2).reshape(tok_count, part)
    moe_out = spread(out_part).transpose(1, 0, 2).reshape(tok_count, width)

    context = attend(queries, previous, group_latent, unit_rows)
    return (context, moe_out)


def solution(mesh):
    return jax.shard_map(
        per_device,
        mesh=mesh,
        in_specs=(
            P("expert", "section", None),
            P("expert", None),
            P("expert", None, None),
            P(),
            P("expert", None),
            P("expert", None),
            P("expert", None),
            P("expert", None, "section"),
            P("expert", None, "section"),
            P("expert", "section", None),
        ),
        out_specs=(P("expert", "section", None), P("expert", None)),
        check_vma=False,
    )
```

```python
import functools

import jax
import jax.numpy as jnp
from jax import lax
from jax.experimental import pallas as pl
from jax.experimental.pallas import tpu as pltpu
from jax.sharding import PartitionSpec as P

LATENT = 512
N_EXPERT = 32
N_SECTION = 8
N_Y = 4
N_Z = 8
N_J = 4
CAP = 10
AUX = 128
AUX_AT = 640
Z_ORDER = (0, 1, 7, 2, 6, 3, 5, 4)
BLOCK = 64

score_scale = 192.0 ** (-0.5)
route_scale = 2.5

J_GROUPS = [[z * N_J + j for j in range(N_J)] for z in range(N_Z)]
Z_GROUPS = [[z * N_J + j for z in range(N_Z)] for j in range(N_J)]

VMEM = pl.BlockSpec(memory_space=pltpu.VMEM)
SMEM = pl.BlockSpec(memory_space=pltpu.SMEM)


def along_y(value, step):
    pairs = [
        (a * N_Y + y, a * N_Y + (y + step) % N_Y) for a in range(2) for y in range(N_Y)
    ]
    return lax.ppermute(value, "section", pairs)


def across_x(value):
    pairs = [(s, (s + N_Y) % N_SECTION) for s in range(N_SECTION)]
    return lax.ppermute(value, "section", pairs)


def across_section(value, bits):
    return lax.ppermute(value, "section", [(s, s ^ bits) for s in range(N_SECTION)])


def across_j(value, bit):
    return lax.ppermute(value, "expert", [(e, e ^ bit) for e in range(N_EXPERT)])


def along_z(value, steps):
    return lax.ppermute(
        value, "expert", [(e, (e + steps * N_J) % N_EXPERT) for e in range(N_EXPERT)]
    )


def over_z(value):
    return lax.all_to_all(
        value, "expert", split_axis=0, concat_axis=0, tiled=True, axis_index_groups=Z_GROUPS
    )


def over_j(value):
    return lax.all_to_all(
        value, "expert", split_axis=0, concat_axis=0, tiled=True, axis_index_groups=J_GROUPS
    )


def over_section(value):
    return lax.all_to_all(value, "section", split_axis=0, concat_axis=0, tiled=True)


def after(value, *others):
    return lax.optimization_barrier((value,) + others)[0]


def cost(flops, moved):
    return pl.CostEstimate(flops=flops, bytes_accessed=moved, transcendentals=0)


def params():
    return pltpu.CompilerParams(vmem_limit_bytes=60 * 1024 * 1024)


def prep_kernel(at_ref, unit_ref, tok_ref, ids_ref, aff_ref, cache_ref, out_ref):
    count, part = tok_ref.shape
    held, unit_len, qk = cache_ref.shape
    own_y, own_e = lax.rem(at_ref[0], N_Y), at_ref[1]
    affinity = aff_ref[...]
    high = affinity.astype(jnp.bfloat16).astype(jnp.float32)
    mid = (affinity - high).astype(jnp.bfloat16).astype(jnp.float32)
    low = affinity - high - mid
    names = jnp.concatenate([ids_ref[...].astype(jnp.float32), high, mid, low], 1)
    out_ref[0:count] = tok_ref[...]
    mine = jnp.int32(0)
    for i in range(unit_ref.shape[0]):
        unit = unit_ref[i]
        mine = mine + jnp.where(unit // held == own_e, unit % held, 0)
    extra = out_ref.shape[0] - count
    cut = unit_len // N_Y
    row = lax.broadcasted_iota(jnp.int32, (extra, unit_len), 0)
    column = lax.broadcasted_iota(jnp.int32, (extra, unit_len), 1)
    pick = jnp.where((column == own_y * cut + row) & (row < cut), 1.0, 0.0).astype(jnp.bfloat16)
    rows = jnp.dot(pick, cache_ref[mine], preferred_element_type=jnp.float32)
    names = jnp.concatenate([names, jnp.zeros((extra - 8, AUX), jnp.float32)], 0)
    rows = jnp.concatenate(
        [
            rows,
            jnp.zeros((extra, AUX_AT - qk), jnp.float32),
            names,
            jnp.zeros((extra, part - AUX_AT - AUX), jnp.float32),
        ],
        1,
    )
    out_ref[count:] = rows.astype(jnp.bfloat16)


def prep(at, unit_ids, tokens_b, expert_ids, affinity, cache_latent):
    count, width = tokens_b.shape
    part = width // N_SECTION
    rows = count + 16
    grid_spec = pltpu.PrefetchScalarGridSpec(
        num_scalar_prefetch=2,
        grid=(1,),
        in_specs=[
            pl.BlockSpec((count, part), lambda i, a, u: (0, a[0])),
            pl.BlockSpec((expert_ids.shape[1], count), lambda i, a, u: (0, 0)),
            pl.BlockSpec((expert_ids.shape[1], count), lambda i, a, u: (0, 0)),
            pl.BlockSpec(cache_latent.shape, lambda i, a, u: (0, 0, 0)),
        ],
        out_specs=pl.BlockSpec((rows, part), lambda i, a, u: (0, 0)),
    )
    return pl.pallas_call(
        prep_kernel,
        grid_spec=grid_spec,
        out_shape=jax.ShapeDtypeStruct((rows, part), jnp.bfloat16),
        compiler_params=params(),
        cost_estimate=cost(1000, 400 * 1024),
        name="prep",
    )(at, unit_ids, tokens_b, expert_ids.T, affinity.T, cache_latent)


def pack_kernel(e_ref, m_ref, c_ref, x_ref, xc_ref, slot_ref, share_ref, *out_refs):
    rows = N_Z * out_refs[0].shape[0]
    count = slot_ref.shape[1] // N_J
    refs = (m_ref, c_ref, x_ref, xc_ref)
    toks = jnp.concatenate([r[0:count, :] for r in refs], 0)
    total = toks.shape[0]
    aux = [r[count:, AUX_AT : AUX_AT + AUX].astype(jnp.float32)[0:8] for r in refs]
    ids, high, mid, low = [
        jnp.concatenate([a[:, k * count : (k + 1) * count] for a in aux], 1) for k in range(4)
    ]
    affinity = high + mid + low
    share = route_scale * affinity / jnp.sum(affinity, 0, keepdims=True)
    named, shares = [], []
    for step in range(N_Z):
        expert = lax.rem(e_ref[0] + step * N_J, N_EXPERT)
        hit = ids == expert.astype(jnp.float32)
        named.append(jnp.sum(jnp.where(hit, 1.0, 0.0), 0, keepdims=True))
        shares.append(jnp.sum(jnp.where(hit, share, 0.0), 0, keepdims=True))
    named = jnp.concatenate(named, 0)
    before = lax.broadcasted_iota(jnp.int32, (total, total), 0)
    later = lax.broadcasted_iota(jnp.int32, (total, total), 1)
    earlier = ((before // count) == (later // count)) & (before < later)
    rank = jnp.dot(
        named.astype(jnp.bfloat16),
        jnp.where(earlier, 1.0, 0.0).astype(jnp.bfloat16),
        preferred_element_type=jnp.float32,
    )
    source = lax.broadcasted_iota(jnp.int32, (N_Z, total), 1) // count
    slot = jnp.where(named > 0.5, rank + (source * CAP).astype(jnp.float32), -1.0)
    slot_ref[...] = slot
    share_ref[...] = jnp.concatenate(shares, 0)
    each = rows // N_Z
    place = lax.broadcasted_iota(jnp.int32, (N_Z, each, total), 1).astype(jnp.float32)
    pick = jnp.where(slot[:, None, :] == place, 1.0, 0.0).reshape(rows, total)
    got = jnp.dot(pick.astype(jnp.bfloat16), toks, preferred_element_type=jnp.float32)
    part = toks.shape[1]
    qk = out_refs[0].shape[1] - part
    units = [r[count:, :qk].astype(jnp.float32)[0:8] for r in refs]
    units = units + [jnp.zeros((each - N_J * 8, qk), jnp.float32)]
    units = jnp.concatenate(units, 0)
    for step, out_ref in enumerate(out_refs):
        rows = jnp.concatenate([got[step * each : (step + 1) * each], units], 1)
        out_ref[...] = rows.astype(jnp.bfloat16)


def pack(own_e, messages, part, qk):
    rows = N_J * CAP
    piece = jax.ShapeDtypeStruct((rows, part + qk), jnp.bfloat16)
    table = jax.ShapeDtypeStruct((N_Z, 128), jnp.float32)
    slot, share, *pieces = pl.pallas_call(
        pack_kernel,
        out_shape=(table,) * 2 + (piece,) * N_Z,
        in_specs=[SMEM] + [VMEM] * 4,
        out_specs=(VMEM,) * (2 + N_Z),
        compiler_params=params(),
        cost_estimate=cost(2 * N_Z * rows * 128 * part, 2 * N_Z * rows * part * 2),
        name="pack",
    )(own_e, *messages)
    return pieces, slot, share


def cut_kernel(in_ref, out_ref):
    part = out_ref.shape[2]
    for k in range(out_ref.shape[0]):
        out_ref[k] = in_ref[0, :, k * part : (k + 1) * part]


def cut_down(down_w):
    _, f, width = down_w.shape
    part = width // N_SECTION
    return pl.pallas_call(
        cut_kernel,
        out_shape=jax.ShapeDtypeStruct((N_SECTION, f, part), jnp.bfloat16),
        in_specs=[VMEM],
        out_specs=VMEM,
        compiler_params=params(),
        cost_estimate=cost(0, 2 * f * width * 2),
        name="cut_down",
    )(down_w)


def whole(shape):
    return pl.BlockSpec(shape, lambda i, s: (0,) * len(shape))


def sum_kernel(places, at_ref, *refs):
    xs, (gate, up, out_ref) = refs[:-3], refs[-3:]
    rows, part = xs[0].shape
    own_x, own_y = at_ref[0] // N_Y, lax.rem(at_ref[0], N_Y)
    total = None
    for b, (dx, dy) in enumerate(places):
        block = jnp.bitwise_xor(own_x, dx) * N_Y + lax.rem(own_y + dy, N_Y)
        k = pl.ds(pl.multiple_of(block * part, part), part)
        weights = jnp.concatenate([gate[0, k], up[0, k]], 1)
        x = jnp.concatenate([xs[2 * b][...], xs[2 * b + 1][...]], 0)
        term = jnp.dot(x, weights, preferred_element_type=jnp.float32)
        total = term if total is None else total + term
    f = out_ref.shape[2]
    gate, up = total[:, :f], total[:, f:]
    hidden = (gate / (1.0 + jnp.exp(-gate)) * up).astype(jnp.bfloat16)
    for s in range(out_ref.shape[0]):
        out_ref[s] = hidden


def add_blocks(at, blocks, gate_w, up_w):
    f = gate_w.shape[2]
    half, part = blocks[0][2][0].shape
    xs = [x for _, _, halves in blocks for x in halves]
    places = tuple((dx, dy) for dx, dy, _ in blocks)
    return pl.pallas_call(
        functools.partial(sum_kernel, places),
        out_shape=jax.ShapeDtypeStruct((N_SECTION, 2 * half, f), jnp.bfloat16),
        in_specs=[SMEM] + [VMEM] * (len(xs) + 2),
        out_specs=VMEM,
        compiler_params=params(),
        cost_estimate=cost(8 * half * part * f * len(blocks), 10 * 1024 * 1024),
        name="add_blocks",
    )(at, *xs, gate_w, up_w)


def down_kernel(e_ref, hid, w_ref, out_ref):
    total = None
    for k in range(0, N_SECTION, 2):
        left = jnp.concatenate([hid[k], hid[k + 1]], 1)
        right = jnp.concatenate([w_ref[k], w_ref[k + 1]], 0)
        term = jnp.dot(left, right, preferred_element_type=jnp.float32)
        total = term if total is None else total + term
    each = out_ref.shape[1]
    own_z = e_ref[0] // N_J
    for i, step in enumerate(Z_ORDER):
        rows = total[i * each : (i + 1) * each].astype(jnp.bfloat16)
        out_ref[lax.rem(own_z + N_Z - step, N_Z)] = rows


def down(own_e, hidden, weights):
    _, rows, f = hidden.shape
    part = weights.shape[2]
    return pl.pallas_call(
        down_kernel,
        out_shape=jax.ShapeDtypeStruct((N_Z, rows // N_Z, part), jnp.bfloat16),
        in_specs=[SMEM] + [VMEM] * 2,
        out_specs=VMEM,
        compiler_params=params(),
        cost_estimate=cost(2 * rows * f * N_SECTION * part, 4 * 1024 * 1024),
        name="down",
    )(own_e, hidden, weights)


def mix_kernel(e_ref, slot_ref, share_ref, back_ref, out_ref):
    rows = back_ref.shape[0]
    own_z, own_j = e_ref[0] // N_J, lax.rem(e_ref[0], N_J)

    def by_z(ref):
        at = [lax.rem(z + N_Z - own_z, N_Z) for z in range(N_Z)]
        return jnp.concatenate([ref[pl.ds(k, 1), :] for k in at], 0)

    each = rows // N_Z
    total = slot_ref.shape[1]
    place = lax.broadcasted_iota(jnp.int32, (N_Z, each, total), 1).astype(jnp.float32)
    weight = jnp.where(by_z(slot_ref)[:, None, :] == place, by_z(share_ref)[:, None, :], 0.0)
    weight = weight.reshape(rows, total)
    high = weight.astype(jnp.bfloat16)
    low = (weight - high.astype(jnp.float32)).astype(jnp.bfloat16)
    back = back_ref[...]
    dims = (((0,), (0,)), ((), ()))
    got = lax.dot_general(high, back, dims, preferred_element_type=jnp.float32)
    got = got + lax.dot_general(low, back, dims, preferred_element_type=jnp.float32)
    count = out_ref.shape[1]
    for p in range(N_J):
        rows = got[p * count : (p + 1) * count].astype(jnp.bfloat16)
        out_ref[jnp.bitwise_xor(own_j, p)] = rows


def mix(own_e, slot, share, back):
    rows, part = back.shape
    count = slot.shape[1] // N_J
    return pl.pallas_call(
        mix_kernel,
        out_shape=jax.ShapeDtypeStruct((N_J, count, part), jnp.bfloat16),
        in_specs=[SMEM] + [VMEM] * 3,
        out_specs=VMEM,
        compiler_params=params(),
        cost_estimate=cost(4 * rows * N_J * count * part, rows * part * 4),
        name="mix",
    )(own_e, slot, share, back)


def attend_kernel(first_step, s_ref, q_ref, prev_ref, own_ref, *refs):
    unit_refs, (out_ref, keys_ref, units_ref) = refs[:N_Y], refs[-3:]
    block, heads = BLOCK, q_ref.shape[0] // BLOCK
    count = own_ref.shape[0]
    step = pl.program_id(0) + first_step

    @pl.when(step == first_step)
    def _():
        keys_ref[0:count] = prev_ref[...]
        keys_ref[count:] = own_ref[...]
        for i, unit_ref in enumerate(unit_refs):
            rows = unit_ref.shape[0]
            units_ref[i * rows : (i + 1) * rows] = unit_ref[...]

    span = count + block
    keys = keys_ref[pl.ds(pl.multiple_of(step * block, block), span), :]
    units = units_ref[...]
    q = q_ref[...]
    dims = (((1,), (1,)), ((), ()))
    win = lax.dot_general(q, keys, dims, preferred_element_type=jnp.float32) * score_scale
    far = lax.dot_general(q, units, dims, preferred_element_type=jnp.float32) * score_scale
    token = lax.broadcasted_iota(jnp.int32, win.shape, 0) // heads
    key = lax.broadcasted_iota(jnp.int32, win.shape, 1)
    first = jnp.where(s_ref[0] == 0, count - step * block, 0)
    allowed = (key > token) & (key <= token + count) & (key >= first)
    win = jnp.where(allowed, win, -1e30)
    top = jnp.maximum(jnp.max(win, 1, keepdims=True), jnp.max(far, 1, keepdims=True))
    win = jnp.exp(win - top)
    far = jnp.exp(far - top)
    denominator = jnp.sum(win, 1, keepdims=True) + jnp.sum(far, 1, keepdims=True)
    got = jnp.dot(win.astype(jnp.bfloat16), keys[:, :LATENT], preferred_element_type=jnp.float32)
    got = got + jnp.dot(
        far.astype(jnp.bfloat16), units[:, :LATENT], preferred_element_type=jnp.float32
    )
    out_ref[...] = (got / denominator).astype(jnp.bfloat16)


def attend(own_e, queries, previous, group_latent, unit_rows, first_step, steps, context=None):
    count, qk = group_latent.shape
    heads = queries.shape[0] // count
    rows = BLOCK * heads
    operands = [queries, previous, group_latent, *unit_rows]
    specs = [pl.BlockSpec((rows, qk), lambda i, s: (i + first_step, 0))]
    specs += [whole(x.shape) for x in operands[1:]]
    aliases = {}
    if context is not None:
        aliases = {1 + len(operands): 0}
        operands.append(context)
        specs.append(pl.BlockSpec(memory_space=pl.ANY))
    return pl.pallas_call(
        functools.partial(attend_kernel, first_step),
        grid_spec=pltpu.PrefetchScalarGridSpec(
            num_scalar_prefetch=1,
            grid=(steps,),
            in_specs=specs,
            out_specs=pl.BlockSpec((rows, LATENT), lambda i, s: (i + first_step, 0)),
            scratch_shapes=[
                pltpu.VMEM((2 * count, qk), jnp.bfloat16),
                pltpu.VMEM((N_Y * unit_rows[0].shape[0], qk), jnp.bfloat16),
            ],
        ),
        out_shape=jax.ShapeDtypeStruct((count * heads, LATENT), jnp.bfloat16),
        input_output_aliases=aliases,
        compiler_params=params(),
        cost_estimate=cost(1000 * 1000 * 1000 * steps, 2 * 1024 * 1024 * steps),
        name="attend",
    )(own_e, *operands)


def per_device(
    queries,
    group_latent,
    cache_latent,
    unit_ids,
    tokens_b,
    expert_ids,
    affinity,
    gate_w,
    up_w,
    down_w,
):
    own_s = lax.axis_index("section")
    own_e = lax.axis_index("expert")
    at = jnp.stack([own_s, own_e]).astype(jnp.int32)
    tok_count, width = tokens_b.shape
    part = width // N_SECTION
    held, unit_len, qk = cache_latent.shape
    cut = unit_len // N_Y

    message = prep(at, unit_ids, tokens_b, expert_ids, affinity, cache_latent)
    messages = (message,) + tuple(across_j(message, bit) for bit in (1, 2, 3))
    previous = lax.ppermute(
        group_latent, "expert", [(i, i + 1) for i in range(N_EXPERT - 1)]
    )

    down_cut = cut_down(after(down_w, message))
    down_all = over_section(after(down_cut, *messages))

    own_e = own_e[None].astype(jnp.int32)
    pieces, slot, share = pack(own_e, messages, part, qk)
    pieces = [piece if step == 0 else along_z(piece, step) for step, piece in enumerate(pieces)]
    pieces = [pieces[step] for step in Z_ORDER]
    first, second = (
        jnp.concatenate([piece[:, :part] for piece in pieces[i : i + 4]], 0) for i in (0, 4)
    )
    units = [piece[: N_J * cut, part:] for piece in pieces]
    first, second = lax.optimization_barrier((first, second, down_all))[:2]

    before_1 = along_y(first, 1)
    after_2 = along_y(second, -1)
    x_1 = across_x(first)
    before_2 = along_y(second, 1)
    after_1 = along_y(first, -1)
    x_2 = across_x(second)
    far_1 = along_y(before_1, 1)
    far_2 = along_y(after_2, -1)
    before_x = [along_y(x_1, 1), along_y(x_2, 1)]
    after_x = [along_y(x_1, -1), along_y(x_2, -1)]

    far_x = [across_x(far_1), across_x(far_2)]
    blocks = [
        (0, 0, [first, second]),
        (0, 3, [before_1, before_2]),
        (0, 1, [after_1, after_2]),
        (1, 0, [x_1, x_2]),
        (0, 2, [far_1, far_2]),
        (1, 3, before_x),
        (1, 1, after_x),
        (1, 2, far_x),
    ]
    hidden = over_section(add_blocks(at, blocks, gate_w, up_w))

    owner = unit_ids // held
    steps = (own_e // N_J - owner // N_J) % N_Z
    steps = jnp.array([Z_ORDER.index(step) for step in range(N_Z)], jnp.int32)[steps]
    order = steps * N_J + ((owner ^ own_e) % N_J)
    units = list(lax.optimization_barrier((*units, hidden))[:-1])
    units = jnp.concatenate(units, 0).reshape(N_Z * N_J, cut, qk)[order].reshape(-1, qk)
    unit_rows = (units, along_y(units, 1), along_y(units, -1), along_y(units, 2))
    back = over_z(down(own_e, hidden, down_all)).reshape(-1, part)

    keys = (previous, group_latent, unit_rows)
    half = group_latent.shape[0] // BLOCK // 2
    back, rows_q, *_ = lax.optimization_barrier(
        (back, queries.reshape(-1, qk), unit_rows, previous)
    )
    context = attend(at[1:], after(rows_q, back), *keys, 0, half)
    mixed = over_j(mix(own_e, slot, share, back))
    mixed, context = lax.optimization_barrier((mixed, context))
    out_part = jnp.sum(mixed.astype(jnp.float32), 0).astype(jnp.bfloat16)
    out_part = jnp.broadcast_to(out_part[None], (N_SECTION, tok_count, part))
    context = attend(at[1:], after(rows_q, mixed), *keys, half, half, context)
    context = context.reshape(queries.shape[0], queries.shape[1], LATENT)
    moe_out = over_section(out_part).transpose(1, 0, 2).reshape(tok_count, width)
    return (context, moe_out)


def solution(mesh):
    return jax.shard_map(
        per_device,
        mesh=mesh,
        in_specs=(
            P("expert", "section", None),
            P("expert", None),
            P("expert", None, None),
            P(),
            P("expert", None),
            P("expert", None),
            P("expert", None),
            P("expert", None, "section"),
            P("expert", None, "section"),
            P("expert", "section", None),
        ),
        out_specs=(P("expert", "section", None), P("expert", None)),
        check_vma=False,
    )
```

```python
import functools

import jax
import jax.numpy as jnp
from jax import lax
from jax.experimental import pallas as pl
from jax.experimental.pallas import tpu as pltpu
from jax.sharding import PartitionSpec as P

LATENT = 512
N_EXPERT = 32
N_SECTION = 8
N_Y = 4
N_Z = 8
N_J = 4
CAP = 10
AUX = 128
AUX_AT = 640
U_HELD = 4
REST = 64
Z_ORDER = (0, 1, 7, 2, 6, 3, 5, 4)
BLOCK = 64

score_scale = 192.0 ** (-0.5)
route_scale = 2.5

Z_GROUPS = [[z * N_J + j for z in range(N_Z)] for j in range(N_J)]

VMEM = pl.BlockSpec(memory_space=pltpu.VMEM)
ANY = pl.BlockSpec(memory_space=pl.ANY)
SMEM = pl.BlockSpec(memory_space=pltpu.SMEM)


def along_y(value, step):
    pairs = [
        (a * N_Y + y, a * N_Y + (y + step) % N_Y) for a in range(2) for y in range(N_Y)
    ]
    return lax.ppermute(value, "section", pairs)


def across_x(value):
    pairs = [(s, (s + N_Y) % N_SECTION) for s in range(N_SECTION)]
    return lax.ppermute(value, "section", pairs)


def across_section(value, bits):
    return lax.ppermute(value, "section", [(s, s ^ bits) for s in range(N_SECTION)])


def across_j(value, bit):
    return lax.ppermute(value, "expert", [(e, e ^ bit) for e in range(N_EXPERT)])


def along_z(value, steps):
    return lax.ppermute(
        value, "expert", [(e, (e + steps * N_J) % N_EXPERT) for e in range(N_EXPERT)]
    )


def over_z(value):
    return lax.all_to_all(
        value, "expert", split_axis=0, concat_axis=0, tiled=True, axis_index_groups=Z_GROUPS
    )


def over_section(value):
    return lax.all_to_all(value, "section", split_axis=0, concat_axis=0, tiled=True)


def after(value, *others):
    return lax.optimization_barrier((value,) + others)[0]


def cost(flops, moved):
    return pl.CostEstimate(flops=flops, bytes_accessed=moved, transcendentals=0)


def params():
    return pltpu.CompilerParams(vmem_limit_bytes=60 * 1024 * 1024)


def prep_kernel(at_ref, unit_ref, tok_ref, ids_ref, aff_ref, cache_ref, out_ref):
    count, part = tok_ref.shape
    held, unit_len, qk = cache_ref.shape
    own_y, own_e = lax.rem(at_ref[0], N_Y), at_ref[1]
    affinity = aff_ref[...]
    high = affinity.astype(jnp.bfloat16).astype(jnp.float32)
    mid = (affinity - high).astype(jnp.bfloat16).astype(jnp.float32)
    low = affinity - high - mid
    names = jnp.concatenate([ids_ref[...].astype(jnp.float32), high, mid, low], 1)
    out_ref[0:count] = tok_ref[...]
    mine = jnp.int32(0)
    for i in range(unit_ref.shape[0]):
        unit = unit_ref[i]
        mine = mine + jnp.where(unit // held == own_e, unit % held, 0)
    extra = out_ref.shape[0] - count
    cut = unit_len // N_Y
    row = lax.broadcasted_iota(jnp.int32, (extra, unit_len), 0)
    column = lax.broadcasted_iota(jnp.int32, (extra, unit_len), 1)
    pick = jnp.where((column == own_y * cut + row) & (row < cut), 1.0, 0.0).astype(jnp.bfloat16)
    rows = jnp.dot(pick, cache_ref[mine], preferred_element_type=jnp.float32)
    names = jnp.concatenate([names, jnp.zeros((extra - 8, AUX), jnp.float32)], 0)
    rows = jnp.concatenate(
        [
            rows,
            jnp.zeros((extra, AUX_AT - qk), jnp.float32),
            names,
            jnp.zeros((extra, part - AUX_AT - AUX), jnp.float32),
        ],
        1,
    )
    out_ref[count:] = rows.astype(jnp.bfloat16)


def prep(at, unit_ids, tokens_b, expert_ids, affinity, cache_latent):
    count, width = tokens_b.shape
    part = width // N_SECTION
    rows = count + 16
    grid_spec = pltpu.PrefetchScalarGridSpec(
        num_scalar_prefetch=2,
        grid=(1,),
        in_specs=[
            pl.BlockSpec((count, part), lambda i, a, u: (0, a[0])),
            pl.BlockSpec((expert_ids.shape[1], count), lambda i, a, u: (0, 0)),
            pl.BlockSpec((expert_ids.shape[1], count), lambda i, a, u: (0, 0)),
            pl.BlockSpec(cache_latent.shape, lambda i, a, u: (0, 0, 0)),
        ],
        out_specs=pl.BlockSpec((rows, part), lambda i, a, u: (0, 0)),
    )
    return pl.pallas_call(
        prep_kernel,
        grid_spec=grid_spec,
        out_shape=jax.ShapeDtypeStruct((rows, part), jnp.bfloat16),
        compiler_params=params(),
        cost_estimate=cost(1000, 400 * 1024),
        name="prep",
    )(at, unit_ids, tokens_b, expert_ids.T, affinity.T, cache_latent)


def pack_kernel(e_ref, m_ref, c_ref, x_ref, xc_ref, slot_ref, share_ref, *out_refs):
    rows = N_Z * out_refs[0].shape[0]
    count = slot_ref.shape[1] // N_J
    refs = (m_ref, c_ref, x_ref, xc_ref)
    toks = jnp.concatenate([r[0:count, :] for r in refs], 0)
    total = toks.shape[0]
    aux = [r[count:, AUX_AT : AUX_AT + AUX].astype(jnp.float32)[0:8] for r in refs]
    ids, high, mid, low = [
        jnp.concatenate([a[:, k * count : (k + 1) * count] for a in aux], 1) for k in range(4)
    ]
    affinity = high + mid + low
    share = route_scale * affinity / jnp.sum(affinity, 0, keepdims=True)
    named, shares = [], []
    for step in range(N_Z):
        expert = lax.rem(e_ref[0] + step * N_J, N_EXPERT)
        hit = ids == expert.astype(jnp.float32)
        named.append(jnp.sum(jnp.where(hit, 1.0, 0.0), 0, keepdims=True))
        shares.append(jnp.sum(jnp.where(hit, share, 0.0), 0, keepdims=True))
    named = jnp.concatenate(named, 0)
    before = lax.broadcasted_iota(jnp.int32, (total, total), 0)
    later = lax.broadcasted_iota(jnp.int32, (total, total), 1)
    earlier = ((before // count) == (later // count)) & (before < later)
    rank = jnp.dot(
        named.astype(jnp.bfloat16),
        jnp.where(earlier, 1.0, 0.0).astype(jnp.bfloat16),
        preferred_element_type=jnp.float32,
    )
    source = lax.broadcasted_iota(jnp.int32, (N_Z, total), 1) // count
    slot = jnp.where(named > 0.5, rank + (source * CAP).astype(jnp.float32), -1.0)
    slot_ref[...] = slot
    share_ref[...] = jnp.concatenate(shares, 0)
    each = rows // N_Z
    place = lax.broadcasted_iota(jnp.int32, (N_Z, each, total), 1).astype(jnp.float32)
    pick = jnp.where(slot[:, None, :] == place, 1.0, 0.0).reshape(rows, total)
    got = jnp.dot(pick.astype(jnp.bfloat16), toks, preferred_element_type=jnp.float32)
    part = toks.shape[1]
    units = [r[count:, :AUX_AT].astype(jnp.float32)[0:8] for r in refs]
    rests = [u[:, LATENT : LATENT + REST] for u in units]
    rests = rests + [jnp.zeros((8, LATENT - N_J * REST), jnp.float32)]
    units = [u[:, :LATENT] for u in units] + [jnp.concatenate(rests, 1)]
    units = jnp.concatenate(units, 0)
    for step, out_ref in enumerate(out_refs):
        rows = jnp.concatenate([got[step * each : (step + 1) * each], units], 1)
        out_ref[...] = rows.astype(jnp.bfloat16)


def pack(own_e, messages, part):
    rows = N_J * CAP
    piece = jax.ShapeDtypeStruct((rows, part + LATENT), jnp.bfloat16)
    table = jax.ShapeDtypeStruct((N_Z, 128), jnp.float32)
    slot, share, *pieces = pl.pallas_call(
        pack_kernel,
        out_shape=(table,) * 2 + (piece,) * N_Z,
        in_specs=[SMEM] + [VMEM] * 4,
        out_specs=(VMEM,) * (2 + N_Z),
        compiler_params=params(),
        cost_estimate=cost(2 * N_Z * rows * 128 * part, 2 * N_Z * rows * part * 2),
        name="pack",
    )(own_e, *messages)
    return pieces, slot, share


def cut_kernel(in_ref, out_ref):
    part = out_ref.shape[2]
    for k in range(out_ref.shape[0]):
        out_ref[k] = in_ref[0, :, k * part : (k + 1) * part]


def cut_down(down_w):
    _, f, width = down_w.shape
    part = width // N_SECTION
    return pl.pallas_call(
        cut_kernel,
        out_shape=jax.ShapeDtypeStruct((N_SECTION, f, part), jnp.bfloat16),
        in_specs=[VMEM],
        out_specs=VMEM,
        compiler_params=params(),
        cost_estimate=cost(0, 2 * f * width * 2),
        name="cut_down",
    )(down_w)


def whole(shape):
    return pl.BlockSpec(shape, lambda i, s: (0,) * len(shape))


def sum_kernel(places, at_ref, *refs):
    count = 2 * len(places)
    xs, (gate, up, out_ref, x_buf, w_buf, x_sem, w_sem) = refs[:count], refs[count:]
    half, part = xs[0].shape
    f = out_ref.shape[2]
    own_x, own_y = at_ref[0] // N_Y, lax.rem(at_ref[0], N_Y)
    copies = []
    for b, (dx, dy) in enumerate(places):
        block = jnp.bitwise_xor(own_x, dx) * N_Y + lax.rem(own_y + dy, N_Y)
        k = pl.ds(pl.multiple_of(block * part, part), part)
        mine = [
            pltpu.make_async_copy(
                xs[2 * b + h], x_buf.at[b, pl.ds(h * half, half)], x_sem.at[2 * b + h]
            )
            for h in range(2)
        ]
        mine += [
            pltpu.make_async_copy(
                ref.at[0, k], w_buf.at[b, :, pl.ds(i * f, f)], w_sem.at[2 * b + i]
            )
            for i, ref in enumerate((gate, up))
        ]
        for copy in mine:
            copy.start()
        copies.append(mine)
    total = None
    for b, mine in enumerate(copies):
        for copy in mine:
            copy.wait()
        term = jnp.dot(x_buf[b], w_buf[b], preferred_element_type=jnp.float32)
        total = term if total is None else total + term
    gate, up = total[:, :f], total[:, f:]
    hidden = (gate / (1.0 + jnp.exp(-gate)) * up).astype(jnp.bfloat16)
    for s in range(out_ref.shape[0]):
        out_ref[s] = hidden


def add_blocks(at, blocks, gate_w, up_w):
    f = gate_w.shape[2]
    half, part = blocks[0][2][0].shape
    xs = [x for _, _, halves in blocks for x in halves]
    places = tuple((dx, dy) for dx, dy, _ in blocks)
    count = len(blocks)
    return pl.pallas_call(
        functools.partial(sum_kernel, places),
        out_shape=jax.ShapeDtypeStruct((N_SECTION, 2 * half, f), jnp.bfloat16),
        in_specs=[SMEM] + [ANY] * (len(xs) + 2),
        out_specs=VMEM,
        scratch_shapes=[
            pltpu.VMEM((count, 2 * half, part), jnp.bfloat16),
            pltpu.VMEM((count, part, 2 * f), jnp.bfloat16),
            pltpu.SemaphoreType.DMA((2 * count,)),
            pltpu.SemaphoreType.DMA((2 * count,)),
        ],
        compiler_params=params(),
        cost_estimate=cost(8 * half * part * f * count, 10 * 1024 * 1024),
        name="add_blocks",
    )(at, *xs, gate_w, up_w)


def down_kernel(e_ref, hid, w_ref, out_ref, h_buf, w_buf, h_sem, w_sem):
    count, _, f = hid.shape
    copies = []
    for k in range(count):
        at = pl.ds(k * f, f)
        mine = (
            pltpu.make_async_copy(hid.at[k], h_buf.at[:, at], h_sem.at[k]),
            pltpu.make_async_copy(w_ref.at[k], w_buf.at[at], w_sem.at[k]),
        )
        for copy in mine:
            copy.start()
        copies += mine
    for copy in copies:
        copy.wait()
    total = jnp.dot(h_buf[...], w_buf[...], preferred_element_type=jnp.float32)
    each = out_ref.shape[1]
    own_z = e_ref[0] // N_J
    for i, step in enumerate(Z_ORDER):
        rows = total[i * each : (i + 1) * each].astype(jnp.bfloat16)
        out_ref[lax.rem(own_z + N_Z - step, N_Z)] = rows


def down(own_e, hidden, weights):
    count, rows, f = hidden.shape
    part = weights.shape[2]
    return pl.pallas_call(
        down_kernel,
        out_shape=jax.ShapeDtypeStruct((N_Z, rows // N_Z, part), jnp.bfloat16),
        in_specs=[SMEM] + [ANY] * 2,
        out_specs=VMEM,
        scratch_shapes=[
            pltpu.VMEM((rows, count * f), jnp.bfloat16),
            pltpu.VMEM((count * f, part), jnp.bfloat16),
            pltpu.SemaphoreType.DMA((count,)),
            pltpu.SemaphoreType.DMA((count,)),
        ],
        compiler_params=params(),
        cost_estimate=cost(2 * rows * f * N_SECTION * part, 4 * 1024 * 1024),
        name="down",
    )(own_e, hidden, weights)


def units_kernel(e_ref, ids_ref, *refs):
    pieces, out_ref = refs[:-1], refs[-1]
    qk = out_ref.shape[1]
    rows = out_ref.shape[0] // ids_ref.shape[0]
    held = N_J * rows
    first = pieces[0].shape[1] - LATENT
    rest = qk - LATENT
    units = []
    for piece in pieces:
        rows_of = piece[:, first:].astype(jnp.float32)
        rests = [rows_of[held:, j * rest : (j + 1) * rest] for j in range(N_J)]
        units.append(jnp.concatenate([rows_of[:held], jnp.concatenate(rests, 0)], 1))
    units = jnp.concatenate(units, 0).astype(jnp.bfloat16)
    own_e = e_ref[0]
    row = lax.broadcasted_iota(jnp.int32, (rows, units.shape[0]), 0)
    column = lax.broadcasted_iota(jnp.int32, (rows, units.shape[0]), 1)
    picks = []
    for i in range(ids_ref.shape[0]):
        owner = ids_ref[i] // U_HELD
        step = lax.rem(own_e // N_J + N_Z - owner // N_J, N_Z)
        place = jnp.int32(0)
        for k, z_step in enumerate(Z_ORDER):
            place = place + jnp.where(step == z_step, k, 0)
        start = (place * N_J + lax.rem(jnp.bitwise_xor(owner, own_e), N_J)) * rows
        picks.append(jnp.where(column == row + start, 1.0, 0.0))
    picks = jnp.concatenate(picks, 0).astype(jnp.bfloat16)
    out_ref[...] = jnp.dot(picks, units, preferred_element_type=jnp.float32).astype(jnp.bfloat16)


def select_units(own_e, unit_ids, pieces, qk):
    return pl.pallas_call(
        units_kernel,
        out_shape=jax.ShapeDtypeStruct((unit_ids.shape[0] * 8, qk), jnp.bfloat16),
        in_specs=[SMEM, SMEM] + [VMEM] * len(pieces),
        out_specs=VMEM,
        compiler_params=params(),
        cost_estimate=cost(1000, 2 * 1024 * 1024),
        name="select_units",
    )(own_e, unit_ids, *pieces)


def mix_kernel(e_ref, slot_ref, share_ref, back_ref, own_ref, *out_refs):
    rows = back_ref.shape[0]
    own_z = e_ref[0] // N_J

    def by_z(ref):
        at = [lax.rem(z + N_Z - own_z, N_Z) for z in range(N_Z)]
        return jnp.concatenate([ref[pl.ds(k, 1), :] for k in at], 0)

    each = rows // N_Z
    total = slot_ref.shape[1]
    place = lax.broadcasted_iota(jnp.int32, (N_Z, each, total), 1).astype(jnp.float32)
    weight = jnp.where(by_z(slot_ref)[:, None, :] == place, by_z(share_ref)[:, None, :], 0.0)
    weight = weight.reshape(rows, total)
    high = weight.astype(jnp.bfloat16)
    low = (weight - high.astype(jnp.float32)).astype(jnp.bfloat16)
    back = back_ref[...]
    dims = (((0,), (0,)), ((), ()))
    got = lax.dot_general(high, back, dims, preferred_element_type=jnp.float32)
    got = got + lax.dot_general(low, back, dims, preferred_element_type=jnp.float32)
    count = own_ref.shape[0]
    own_ref[...] = got[:count]
    for p, out_ref in enumerate(out_refs, 1):
        out_ref[...] = got[p * count : (p + 1) * count].astype(jnp.bfloat16)


def mix(own_e, slot, share, back):
    rows, part = back.shape
    count = slot.shape[1] // N_J
    return pl.pallas_call(
        mix_kernel,
        out_shape=(jax.ShapeDtypeStruct((count, part), jnp.float32),)
        + (jax.ShapeDtypeStruct((count, part), jnp.bfloat16),) * (N_J - 1),
        in_specs=[SMEM] + [VMEM] * 3,
        out_specs=(VMEM,) * N_J,
        compiler_params=params(),
        cost_estimate=cost(4 * rows * N_J * count * part, rows * part * 4),
        name="mix",
    )(own_e, slot, share, back)


def attend_kernel(first_step, s_ref, q_ref, prev_ref, own_ref, *refs):
    unit_refs, (out_ref, keys_ref, units_ref) = refs[:N_Y], refs[-3:]
    block, heads = BLOCK, q_ref.shape[0] // BLOCK
    count = own_ref.shape[0]
    step = pl.program_id(0) + first_step

    @pl.when(step == first_step)
    def _():
        keys_ref[0:count] = prev_ref[...]
        keys_ref[count:] = own_ref[...]
        for i, unit_ref in enumerate(unit_refs):
            rows = unit_ref.shape[0]
            units_ref[i * rows : (i + 1) * rows] = unit_ref[...]

    span = count + block
    keys = keys_ref[pl.ds(pl.multiple_of(step * block, block), span), :]
    units = units_ref[...]
    q = q_ref[...]
    dims = (((1,), (1,)), ((), ()))
    win = lax.dot_general(q, keys, dims, preferred_element_type=jnp.float32) * score_scale
    far = lax.dot_general(q, units, dims, preferred_element_type=jnp.float32) * score_scale
    token = lax.broadcasted_iota(jnp.int32, win.shape, 0) // heads
    key = lax.broadcasted_iota(jnp.int32, win.shape, 1)
    first = jnp.where(s_ref[0] == 0, count - step * block, 0)
    allowed = (key > token) & (key <= token + count) & (key >= first)
    win = jnp.where(allowed, win, -1e30)
    top = jnp.maximum(jnp.max(win, 1, keepdims=True), jnp.max(far, 1, keepdims=True))
    win = jnp.exp(win - top)
    far = jnp.exp(far - top)
    denominator = jnp.sum(win, 1, keepdims=True) + jnp.sum(far, 1, keepdims=True)
    got = jnp.dot(win.astype(jnp.bfloat16), keys[:, :LATENT], preferred_element_type=jnp.float32)
    got = got + jnp.dot(
        far.astype(jnp.bfloat16), units[:, :LATENT], preferred_element_type=jnp.float32
    )
    out_ref[...] = (got / denominator).astype(jnp.bfloat16)


def attend(own_e, queries, previous, group_latent, unit_rows, first_step, steps, context=None):
    count, qk = group_latent.shape
    heads = queries.shape[0] // count
    rows = BLOCK * heads
    operands = [queries, previous, group_latent, *unit_rows]
    specs = [pl.BlockSpec((rows, qk), lambda i, s: (i + first_step, 0))]
    specs += [whole(x.shape) for x in operands[1:]]
    aliases = {}
    if context is not None:
        aliases = {1 + len(operands): 0}
        operands.append(context)
        specs.append(pl.BlockSpec(memory_space=pl.ANY))
    return pl.pallas_call(
        functools.partial(attend_kernel, first_step),
        grid_spec=pltpu.PrefetchScalarGridSpec(
            num_scalar_prefetch=1,
            grid=(steps,),
            in_specs=specs,
            out_specs=pl.BlockSpec((rows, LATENT), lambda i, s: (i + first_step, 0)),
            scratch_shapes=[
                pltpu.VMEM((2 * count, qk), jnp.bfloat16),
                pltpu.VMEM((N_Y * unit_rows[0].shape[0], qk), jnp.bfloat16),
            ],
        ),
        out_shape=jax.ShapeDtypeStruct((count * heads, LATENT), jnp.bfloat16),
        input_output_aliases=aliases,
        compiler_params=params(),
        cost_estimate=cost(1000 * 1000 * 1000 * steps, 2 * 1024 * 1024 * steps),
        name="attend",
    )(own_e, *operands)


def per_device(
    queries,
    group_latent,
    cache_latent,
    unit_ids,
    tokens_b,
    expert_ids,
    affinity,
    gate_w,
    up_w,
    down_w,
):
    own_s = lax.axis_index("section")
    own_e = lax.axis_index("expert")
    at = jnp.stack([own_s, own_e]).astype(jnp.int32)
    tok_count, width = tokens_b.shape
    part = width // N_SECTION
    qk = cache_latent.shape[2]

    message = prep(at, unit_ids, tokens_b, expert_ids, affinity, cache_latent)
    messages = (message,) + tuple(across_j(message, bit) for bit in (1, 2, 3))
    previous = lax.ppermute(
        group_latent, "expert", [(i, i + 1) for i in range(N_EXPERT - 1)]
    )

    down_cut = cut_down(after(down_w, message))
    down_all = over_section(after(down_cut, *messages))

    own_e = own_e[None].astype(jnp.int32)
    pieces, slot, share = pack(own_e, messages, part)
    pieces = [along_z(pieces[step], step) if step else pieces[step] for step in Z_ORDER]
    first, second = (
        jnp.concatenate([piece[:, :part] for piece in pieces[i : i + 4]], 0) for i in (0, 4)
    )
    second = after(second, down_all)

    before_1 = along_y(first, 1)
    after_2 = along_y(second, -1)
    x_1 = across_x(first)
    before_2 = along_y(second, 1)
    after_1 = along_y(first, -1)
    x_2 = across_x(second)
    far_1 = along_y(before_1, 1)
    far_2 = along_y(after_2, -1)
    before_x = [along_y(x_1, 1), along_y(x_2, 1)]
    after_x = [along_y(x_1, -1), along_y(x_2, -1)]

    far_x = [across_x(far_1), across_x(far_2)]
    blocks = [
        (0, 0, [first, second]),
        (0, 3, [before_1, before_2]),
        (0, 1, [after_1, after_2]),
        (1, 0, [x_1, x_2]),
        (0, 2, [far_1, far_2]),
        (1, 3, before_x),
        (1, 1, after_x),
        (1, 2, far_x),
    ]
    hidden = over_section(add_blocks(at, blocks, gate_w, up_w))

    units = select_units(own_e, unit_ids, pieces, qk)
    hidden, rows_q, units = lax.optimization_barrier(
        (hidden, queries.reshape(-1, qk), units)
    )
    unit_rows = (units, along_y(units, 1), along_y(units, -1), along_y(units, 2))
    back = over_z(down(own_e, hidden, down_all)).reshape(-1, part)

    keys = (previous, group_latent, unit_rows)
    half = group_latent.shape[0] // BLOCK // 2
    back, *_ = lax.optimization_barrier((back, unit_rows, previous))
    context = attend(at[1:], after(rows_q, back), *keys, 0, half)
    kept, *passed = mix(own_e, slot, share, back)
    passed = [across_j(value, bit) for bit, value in enumerate(passed, 1)]
    passed, context = lax.optimization_barrier((passed, context))
    out_part = kept + sum(value.astype(jnp.float32) for value in passed)
    out_part = out_part.astype(jnp.bfloat16)
    out_part = jnp.broadcast_to(out_part[None], (N_SECTION, tok_count, part))
    context = attend(at[1:], after(rows_q, *passed), *keys, half, half, context)
    context = context.reshape(queries.shape[0], queries.shape[1], LATENT)
    moe_out = over_section(out_part).transpose(1, 0, 2).reshape(tok_count, width)
    return (context, moe_out)


def solution(mesh):
    return jax.shard_map(
        per_device,
        mesh=mesh,
        in_specs=(
            P("expert", "section", None),
            P("expert", None),
            P("expert", None, None),
            P(),
            P("expert", None),
            P("expert", None),
            P("expert", None),
            P("expert", None, "section"),
            P("expert", None, "section"),
            P("expert", "section", None),
        ),
        out_specs=(P("expert", "section", None), P("expert", None)),
        check_vma=False,
    )
```

```python
import functools

import jax
import jax.numpy as jnp
from jax import lax
from jax.experimental import pallas as pl
from jax.experimental.pallas import tpu as pltpu
from jax.sharding import PartitionSpec as P

LATENT = 512
N_EXPERT = 32
N_SECTION = 8
N_Y = 4
N_Z = 8
N_J = 4
CAP = 10
AUX = 128
AUX_AT = 640
U_HELD = 4
REST = 64
Z_ORDER = (0, 1, 7, 2, 6, 3, 5, 4)
BLOCK = 64

score_scale = 192.0 ** (-0.5)
route_scale = 2.5

Z_GROUPS = [[z * N_J + j for z in range(N_Z)] for j in range(N_J)]

VMEM = pl.BlockSpec(memory_space=pltpu.VMEM)
ANY = pl.BlockSpec(memory_space=pl.ANY)
SMEM = pl.BlockSpec(memory_space=pltpu.SMEM)


def along_y(value, step):
    pairs = [
        (a * N_Y + y, a * N_Y + (y + step) % N_Y) for a in range(2) for y in range(N_Y)
    ]
    return lax.ppermute(value, "section", pairs)


def across_x(value):
    pairs = [(s, (s + N_Y) % N_SECTION) for s in range(N_SECTION)]
    return lax.ppermute(value, "section", pairs)


def across_section(value, bits):
    return lax.ppermute(value, "section", [(s, s ^ bits) for s in range(N_SECTION)])


def across_j(value, bit):
    return lax.ppermute(value, "expert", [(e, e ^ bit) for e in range(N_EXPERT)])


def along_z(value, steps):
    return lax.ppermute(
        value, "expert", [(e, (e + steps * N_J) % N_EXPERT) for e in range(N_EXPERT)]
    )


def over_z(value):
    return lax.all_to_all(
        value, "expert", split_axis=0, concat_axis=0, tiled=True, axis_index_groups=Z_GROUPS
    )


def over_section(value):
    return lax.all_to_all(value, "section", split_axis=0, concat_axis=0, tiled=True)


def after(value, *others):
    return lax.optimization_barrier((value,) + others)[0]


def cost(flops, moved):
    return pl.CostEstimate(flops=flops, bytes_accessed=moved, transcendentals=0)


def params():
    return pltpu.CompilerParams(vmem_limit_bytes=60 * 1024 * 1024)


def prep_kernel(at_ref, unit_ref, tok_ref, ids_ref, aff_ref, cache_ref, out_ref):
    count, part = tok_ref.shape
    held, unit_len, qk = cache_ref.shape
    own_y, own_e = lax.rem(at_ref[0], N_Y), at_ref[1]
    affinity = aff_ref[...]
    high = affinity.astype(jnp.bfloat16).astype(jnp.float32)
    mid = (affinity - high).astype(jnp.bfloat16).astype(jnp.float32)
    low = affinity - high - mid
    names = jnp.concatenate([ids_ref[...].astype(jnp.float32), high, mid, low], 1)
    out_ref[0:count] = tok_ref[...]
    mine = jnp.int32(0)
    for i in range(unit_ref.shape[0]):
        unit = unit_ref[i]
        mine = mine + jnp.where(unit // held == own_e, unit % held, 0)
    extra = out_ref.shape[0] - count
    cut = unit_len // N_Y
    row = lax.broadcasted_iota(jnp.int32, (extra, unit_len), 0)
    column = lax.broadcasted_iota(jnp.int32, (extra, unit_len), 1)
    pick = jnp.where((column == own_y * cut + row) & (row < cut), 1.0, 0.0).astype(jnp.bfloat16)
    rows = jnp.dot(pick, cache_ref[mine], preferred_element_type=jnp.float32)
    names = jnp.concatenate([names, jnp.zeros((extra - 8, AUX), jnp.float32)], 0)
    rows = jnp.concatenate(
        [
            rows,
            jnp.zeros((extra, AUX_AT - qk), jnp.float32),
            names,
            jnp.zeros((extra, part - AUX_AT - AUX), jnp.float32),
        ],
        1,
    )
    out_ref[count:] = rows.astype(jnp.bfloat16)


def prep(at, unit_ids, tokens_b, expert_ids, affinity, cache_latent):
    count, width = tokens_b.shape
    part = width // N_SECTION
    rows = count + 16
    grid_spec = pltpu.PrefetchScalarGridSpec(
        num_scalar_prefetch=2,
        grid=(1,),
        in_specs=[
            pl.BlockSpec((count, part), lambda i, a, u: (0, a[0])),
            pl.BlockSpec((expert_ids.shape[1], count), lambda i, a, u: (0, 0)),
            pl.BlockSpec((expert_ids.shape[1], count), lambda i, a, u: (0, 0)),
            pl.BlockSpec(cache_latent.shape, lambda i, a, u: (0, 0, 0)),
        ],
        out_specs=pl.BlockSpec((rows, part), lambda i, a, u: (0, 0)),
    )
    return pl.pallas_call(
        prep_kernel,
        grid_spec=grid_spec,
        out_shape=jax.ShapeDtypeStruct((rows, part), jnp.bfloat16),
        compiler_params=params(),
        cost_estimate=cost(1000, 400 * 1024),
        name="prep",
    )(at, unit_ids, tokens_b, expert_ids.T, affinity.T, cache_latent)


def pack_kernel(e_ref, m_ref, c_ref, x_ref, xc_ref, slot_ref, share_ref, *out_refs):
    rows = N_Z * out_refs[0].shape[0]
    count = slot_ref.shape[1] // N_J
    refs = (m_ref, c_ref, x_ref, xc_ref)
    toks = jnp.concatenate([r[0:count, :] for r in refs], 0)
    total = toks.shape[0]
    aux = [r[count:, AUX_AT : AUX_AT + AUX].astype(jnp.float32)[0:8] for r in refs]
    ids, high, mid, low = [
        jnp.concatenate([a[:, k * count : (k + 1) * count] for a in aux], 1) for k in range(4)
    ]
    affinity = high + mid + low
    share = route_scale * affinity / jnp.sum(affinity, 0, keepdims=True)
    named, shares = [], []
    for step in range(N_Z):
        expert = lax.rem(e_ref[0] + step * N_J, N_EXPERT)
        hit = ids == expert.astype(jnp.float32)
        named.append(jnp.sum(jnp.where(hit, 1.0, 0.0), 0, keepdims=True))
        shares.append(jnp.sum(jnp.where(hit, share, 0.0), 0, keepdims=True))
    named = jnp.concatenate(named, 0)
    before = lax.broadcasted_iota(jnp.int32, (total, total), 0)
    later = lax.broadcasted_iota(jnp.int32, (total, total), 1)
    earlier = ((before // count) == (later // count)) & (before < later)
    rank = jnp.dot(
        named.astype(jnp.bfloat16),
        jnp.where(earlier, 1.0, 0.0).astype(jnp.bfloat16),
        preferred_element_type=jnp.float32,
    )
    source = lax.broadcasted_iota(jnp.int32, (N_Z, total), 1) // count
    slot = jnp.where(named > 0.5, rank + (source * CAP).astype(jnp.float32), -1.0)
    slot_ref[...] = slot
    share_ref[...] = jnp.concatenate(shares, 0)
    each = rows // N_Z
    place = lax.broadcasted_iota(jnp.int32, (N_Z, each, total), 1).astype(jnp.float32)
    pick = jnp.where(slot[:, None, :] == place, 1.0, 0.0).reshape(rows, total)
    got = jnp.dot(pick.astype(jnp.bfloat16), toks, preferred_element_type=jnp.float32)
    part = toks.shape[1]
    units = [r[count:, :AUX_AT].astype(jnp.float32)[0:8] for r in refs]
    rests = [u[:, LATENT : LATENT + REST] for u in units]
    rests = rests + [jnp.zeros((8, LATENT - N_J * REST), jnp.float32)]
    units = [u[:, :LATENT] for u in units] + [jnp.concatenate(rests, 1)]
    units = jnp.concatenate(units, 0)
    for step, out_ref in enumerate(out_refs):
        rows = jnp.concatenate([got[step * each : (step + 1) * each], units], 1)
        out_ref[...] = rows.astype(jnp.bfloat16)


def pack(own_e, messages, part):
    rows = N_J * CAP
    piece = jax.ShapeDtypeStruct((rows, part + LATENT), jnp.bfloat16)
    table = jax.ShapeDtypeStruct((N_Z, 128), jnp.float32)
    slot, share, *pieces = pl.pallas_call(
        pack_kernel,
        out_shape=(table,) * 2 + (piece,) * N_Z,
        in_specs=[SMEM] + [VMEM] * 4,
        out_specs=(VMEM,) * (2 + N_Z),
        compiler_params=params(),
        cost_estimate=cost(2 * N_Z * rows * 128 * part, 2 * N_Z * rows * part * 2),
        name="pack",
    )(own_e, *messages)
    return pieces, slot, share


def cut_kernel(in_ref, out_ref):
    part = out_ref.shape[2]
    for k in range(out_ref.shape[0]):
        out_ref[k] = in_ref[0, :, k * part : (k + 1) * part]


def cut_down(down_w):
    _, f, width = down_w.shape
    part = width // N_SECTION
    return pl.pallas_call(
        cut_kernel,
        out_shape=jax.ShapeDtypeStruct((N_SECTION, f, part), jnp.bfloat16),
        in_specs=[VMEM],
        out_specs=VMEM,
        compiler_params=params(),
        cost_estimate=cost(0, 2 * f * width * 2),
        name="cut_down",
    )(down_w)


def whole(shape):
    return pl.BlockSpec(shape, lambda i, s: (0,) * len(shape))


def sum_kernel(places, at_ref, *refs):
    xs, (gate, up, out_ref) = refs[:-3], refs[-3:]
    rows, part = xs[0].shape
    own_x, own_y = at_ref[0] // N_Y, lax.rem(at_ref[0], N_Y)
    total = None
    for b, (dx, dy) in enumerate(places):
        block = jnp.bitwise_xor(own_x, dx) * N_Y + lax.rem(own_y + dy, N_Y)
        k = pl.ds(pl.multiple_of(block * part, part), part)
        weights = jnp.concatenate([gate[0, k], up[0, k]], 1)
        x = jnp.concatenate([xs[2 * b][...], xs[2 * b + 1][...]], 0)
        term = jnp.dot(x, weights, preferred_element_type=jnp.float32)
        total = term if total is None else total + term
    f = out_ref.shape[2]
    gate, up = total[:, :f], total[:, f:]
    hidden = (gate / (1.0 + jnp.exp(-gate)) * up).astype(jnp.bfloat16)
    for s in range(out_ref.shape[0]):
        out_ref[s] = hidden


def add_blocks(at, blocks, gate_w, up_w):
    f = gate_w.shape[2]
    half, part = blocks[0][2][0].shape
    xs = [x for _, _, halves in blocks for x in halves]
    places = tuple((dx, dy) for dx, dy, _ in blocks)
    return pl.pallas_call(
        functools.partial(sum_kernel, places),
        out_shape=jax.ShapeDtypeStruct((N_SECTION, 2 * half, f), jnp.bfloat16),
        in_specs=[SMEM] + [VMEM] * (len(xs) + 2),
        out_specs=VMEM,
        compiler_params=params(),
        cost_estimate=cost(8 * half * part * f * len(blocks), 10 * 1024 * 1024),
        name="add_blocks",
    )(at, *xs, gate_w, up_w)


def down_kernel(e_ref, hid, w_ref, out_ref, h_buf, w_buf, h_sem, w_sem):
    count, _, f = hid.shape
    copies = []
    for k in range(count):
        at = pl.ds(k * f, f)
        mine = (
            pltpu.make_async_copy(hid.at[k], h_buf.at[:, at], h_sem.at[k]),
            pltpu.make_async_copy(w_ref.at[k], w_buf.at[at], w_sem.at[k]),
        )
        for copy in mine:
            copy.start()
        copies += mine
    for copy in copies:
        copy.wait()
    total = jnp.dot(h_buf[...], w_buf[...], preferred_element_type=jnp.float32)
    each = out_ref.shape[1]
    own_z = e_ref[0] // N_J
    for i, step in enumerate(Z_ORDER):
        rows = total[i * each : (i + 1) * each].astype(jnp.bfloat16)
        out_ref[lax.rem(own_z + N_Z - step, N_Z)] = rows


def down(own_e, hidden, weights):
    count, rows, f = hidden.shape
    part = weights.shape[2]
    return pl.pallas_call(
        down_kernel,
        out_shape=jax.ShapeDtypeStruct((N_Z, rows // N_Z, part), jnp.bfloat16),
        in_specs=[SMEM] + [ANY] * 2,
        out_specs=VMEM,
        scratch_shapes=[
            pltpu.VMEM((rows, count * f), jnp.bfloat16),
            pltpu.VMEM((count * f, part), jnp.bfloat16),
            pltpu.SemaphoreType.DMA((count,)),
            pltpu.SemaphoreType.DMA((count,)),
        ],
        compiler_params=params(),
        cost_estimate=cost(2 * rows * f * N_SECTION * part, 4 * 1024 * 1024),
        name="down",
    )(own_e, hidden, weights)


def units_kernel(e_ref, ids_ref, *refs):
    pieces, out_ref = refs[:-1], refs[-1]
    qk = out_ref.shape[1]
    rows = out_ref.shape[0] // ids_ref.shape[0]
    held = N_J * rows
    first = pieces[0].shape[1] - LATENT
    rest = qk - LATENT
    units = []
    for piece in pieces:
        rows_of = piece[:, first:].astype(jnp.float32)
        rests = [rows_of[held:, j * rest : (j + 1) * rest] for j in range(N_J)]
        units.append(jnp.concatenate([rows_of[:held], jnp.concatenate(rests, 0)], 1))
    units = jnp.concatenate(units, 0).astype(jnp.bfloat16)
    own_e = e_ref[0]
    row = lax.broadcasted_iota(jnp.int32, (rows, units.shape[0]), 0)
    column = lax.broadcasted_iota(jnp.int32, (rows, units.shape[0]), 1)
    picks = []
    for i in range(ids_ref.shape[0]):
        owner = ids_ref[i] // U_HELD
        step = lax.rem(own_e // N_J + N_Z - owner // N_J, N_Z)
        place = jnp.int32(0)
        for k, z_step in enumerate(Z_ORDER):
            place = place + jnp.where(step == z_step, k, 0)
        start = (place * N_J + lax.rem(jnp.bitwise_xor(owner, own_e), N_J)) * rows
        picks.append(jnp.where(column == row + start, 1.0, 0.0))
    picks = jnp.concatenate(picks, 0).astype(jnp.bfloat16)
    out_ref[...] = jnp.dot(picks, units, preferred_element_type=jnp.float32).astype(jnp.bfloat16)


def select_units(own_e, unit_ids, pieces, qk):
    return pl.pallas_call(
        units_kernel,
        out_shape=jax.ShapeDtypeStruct((unit_ids.shape[0] * 8, qk), jnp.bfloat16),
        in_specs=[SMEM, SMEM] + [VMEM] * len(pieces),
        out_specs=VMEM,
        compiler_params=params(),
        cost_estimate=cost(1000, 2 * 1024 * 1024),
        name="select_units",
    )(own_e, unit_ids, *pieces)


def mix_kernel(e_ref, slot_ref, share_ref, back_ref, own_ref, *out_refs):
    rows = back_ref.shape[0]
    own_z = e_ref[0] // N_J

    def by_z(ref):
        at = [lax.rem(z + N_Z - own_z, N_Z) for z in range(N_Z)]
        return jnp.concatenate([ref[pl.ds(k, 1), :] for k in at], 0)

    each = rows // N_Z
    total = slot_ref.shape[1]
    place = lax.broadcasted_iota(jnp.int32, (N_Z, each, total), 1).astype(jnp.float32)
    weight = jnp.where(by_z(slot_ref)[:, None, :] == place, by_z(share_ref)[:, None, :], 0.0)
    weight = weight.reshape(rows, total)
    high = weight.astype(jnp.bfloat16)
    low = (weight - high.astype(jnp.float32)).astype(jnp.bfloat16)
    back = back_ref[...]
    dims = (((0,), (0,)), ((), ()))
    got = lax.dot_general(high, back, dims, preferred_element_type=jnp.float32)
    got = got + lax.dot_general(low, back, dims, preferred_element_type=jnp.float32)
    count = own_ref.shape[0]
    own_ref[...] = got[:count]
    for p, out_ref in enumerate(out_refs, 1):
        out_ref[...] = got[p * count : (p + 1) * count].astype(jnp.bfloat16)


def mix(own_e, slot, share, back):
    rows, part = back.shape
    count = slot.shape[1] // N_J
    return pl.pallas_call(
        mix_kernel,
        out_shape=(jax.ShapeDtypeStruct((count, part), jnp.float32),)
        + (jax.ShapeDtypeStruct((count, part), jnp.bfloat16),) * (N_J - 1),
        in_specs=[SMEM] + [VMEM] * 3,
        out_specs=(VMEM,) * N_J,
        compiler_params=params(),
        cost_estimate=cost(4 * rows * N_J * count * part, rows * part * 4),
        name="mix",
    )(own_e, slot, share, back)


def attend_kernel(first_step, s_ref, q_ref, prev_ref, own_ref, *refs):
    unit_refs, (out_ref, keys_ref, units_ref) = refs[:N_Y], refs[-3:]
    block, heads = BLOCK, q_ref.shape[0] // BLOCK
    count = own_ref.shape[0]
    step = pl.program_id(0) + first_step

    @pl.when(step == first_step)
    def _():
        keys_ref[0:count] = prev_ref[...]
        keys_ref[count:] = own_ref[...]
        for i, unit_ref in enumerate(unit_refs):
            rows = unit_ref.shape[0]
            units_ref[i * rows : (i + 1) * rows] = unit_ref[...]

    span = count + block
    keys = keys_ref[pl.ds(pl.multiple_of(step * block, block), span), :]
    units = units_ref[...]
    q = q_ref[...]
    dims = (((1,), (1,)), ((), ()))
    win = lax.dot_general(q, keys, dims, preferred_element_type=jnp.float32) * score_scale
    far = lax.dot_general(q, units, dims, preferred_element_type=jnp.float32) * score_scale
    token = lax.broadcasted_iota(jnp.int32, win.shape, 0) // heads
    key = lax.broadcasted_iota(jnp.int32, win.shape, 1)
    first = jnp.where(s_ref[0] == 0, count - step * block, 0)
    allowed = (key > token) & (key <= token + count) & (key >= first)
    win = jnp.where(allowed, win, -1e30)
    top = jnp.maximum(jnp.max(win, 1, keepdims=True), jnp.max(far, 1, keepdims=True))
    win = jnp.exp(win - top)
    far = jnp.exp(far - top)
    denominator = jnp.sum(win, 1, keepdims=True) + jnp.sum(far, 1, keepdims=True)
    got = jnp.dot(win.astype(jnp.bfloat16), keys[:, :LATENT], preferred_element_type=jnp.float32)
    got = got + jnp.dot(
        far.astype(jnp.bfloat16), units[:, :LATENT], preferred_element_type=jnp.float32
    )
    out_ref[...] = (got / denominator).astype(jnp.bfloat16)


def attend(own_e, queries, previous, group_latent, unit_rows, first_step, steps, context=None):
    count, qk = group_latent.shape
    heads = queries.shape[0] // count
    rows = BLOCK * heads
    operands = [queries, previous, group_latent, *unit_rows]
    specs = [pl.BlockSpec((rows, qk), lambda i, s: (i + first_step, 0))]
    specs += [whole(x.shape) for x in operands[1:]]
    aliases = {}
    if context is not None:
        aliases = {1 + len(operands): 0}
        operands.append(context)
        specs.append(pl.BlockSpec(memory_space=pl.ANY))
    return pl.pallas_call(
        functools.partial(attend_kernel, first_step),
        grid_spec=pltpu.PrefetchScalarGridSpec(
            num_scalar_prefetch=1,
            grid=(steps,),
            in_specs=specs,
            out_specs=pl.BlockSpec((rows, LATENT), lambda i, s: (i + first_step, 0)),
            scratch_shapes=[
                pltpu.VMEM((2 * count, qk), jnp.bfloat16),
                pltpu.VMEM((N_Y * unit_rows[0].shape[0], qk), jnp.bfloat16),
            ],
        ),
        out_shape=jax.ShapeDtypeStruct((count * heads, LATENT), jnp.bfloat16),
        input_output_aliases=aliases,
        compiler_params=params(),
        cost_estimate=cost(1000 * 1000 * 1000 * steps, 2 * 1024 * 1024 * steps),
        name="attend",
    )(own_e, *operands)


def per_device(
    queries,
    group_latent,
    cache_latent,
    unit_ids,
    tokens_b,
    expert_ids,
    affinity,
    gate_w,
    up_w,
    down_w,
):
    own_s = lax.axis_index("section")
    own_e = lax.axis_index("expert")
    at = jnp.stack([own_s, own_e]).astype(jnp.int32)
    tok_count, width = tokens_b.shape
    part = width // N_SECTION
    qk = cache_latent.shape[2]

    message = prep(at, unit_ids, tokens_b, expert_ids, affinity, cache_latent)
    messages = (message,) + tuple(across_j(message, bit) for bit in (1, 2, 3))
    previous = lax.ppermute(
        group_latent, "expert", [(i, i + 1) for i in range(N_EXPERT - 1)]
    )

    down_cut = cut_down(after(down_w, message))
    down_all = over_section(after(down_cut, *messages))

    own_e = own_e[None].astype(jnp.int32)
    pieces, slot, share = pack(own_e, messages, part)
    pieces = [along_z(pieces[step], step) if step else pieces[step] for step in Z_ORDER]
    first, second = (
        jnp.concatenate([piece[:, :part] for piece in pieces[i : i + 4]], 0) for i in (0, 4)
    )
    second = after(second, down_all)

    before_1 = along_y(first, 1)
    after_2 = along_y(second, -1)
    x_1 = across_x(first)
    before_2 = along_y(second, 1)
    after_1 = along_y(first, -1)
    x_2 = across_x(second)
    far_1 = along_y(before_1, 1)
    far_2 = along_y(after_2, -1)
    before_x = [along_y(x_1, 1), along_y(x_2, 1)]
    after_x = [along_y(x_1, -1), along_y(x_2, -1)]

    far_x = [across_x(far_1), across_x(far_2)]
    blocks = [
        (0, 0, [first, second]),
        (0, 3, [before_1, before_2]),
        (0, 1, [after_1, after_2]),
        (1, 0, [x_1, x_2]),
        (0, 2, [far_1, far_2]),
        (1, 3, before_x),
        (1, 1, after_x),
        (1, 2, far_x),
    ]
    hidden = over_section(add_blocks(at, blocks, gate_w, up_w))

    units = select_units(own_e, unit_ids, pieces, qk)
    hidden, rows_q, units = lax.optimization_barrier(
        (hidden, queries.reshape(-1, qk), units)
    )
    unit_rows = (units, along_y(units, 1), along_y(units, -1), along_y(units, 2))
    back = over_z(down(own_e, hidden, down_all)).reshape(-1, part)

    keys = (previous, group_latent, unit_rows)
    steps = group_latent.shape[0] // BLOCK
    back, *_ = lax.optimization_barrier((back, unit_rows, previous))
    context = attend(at[1:], after(rows_q, back), *keys, 0, 1)
    kept, *passed = mix(own_e, slot, share, back)
    passed = [across_j(value, bit) for bit, value in enumerate(passed, 1)]
    passed, context = lax.optimization_barrier((passed, context))
    out_part = kept + sum(value.astype(jnp.float32) for value in passed)
    out_part = out_part.astype(jnp.bfloat16)
    out_part = jnp.broadcast_to(out_part[None], (N_SECTION, tok_count, part))
    context = attend(at[1:], after(rows_q, *passed), *keys, 1, steps - 1, context)
    context = context.reshape(queries.shape[0], queries.shape[1], LATENT)
    moe_out = over_section(out_part).transpose(1, 0, 2).reshape(tok_count, width)
    return (context, moe_out)


def solution(mesh):
    return jax.shard_map(
        per_device,
        mesh=mesh,
        in_specs=(
            P("expert", "section", None),
            P("expert", None),
            P("expert", None, None),
            P(),
            P("expert", None),
            P("expert", None),
            P("expert", None),
            P("expert", None, "section"),
            P("expert", None, "section"),
            P("expert", "section", None),
        ),
        out_specs=(P("expert", "section", None), P("expert", None)),
        check_vma=False,
    )
```

```python
import functools

import jax
import jax.numpy as jnp
from jax import lax
from jax.experimental import pallas as pl
from jax.experimental.pallas import tpu as pltpu
from jax.sharding import PartitionSpec as P

LATENT = 512
N_EXPERT = 32
N_SECTION = 8
N_Y = 4
N_Z = 8
N_J = 4
CAP = 10
AUX = 128
AUX_AT = 640
U_HELD = 4
REST = 64
Z_ORDER = (0, 1, 7, 2, 6, 3, 5, 4)
BLOCK = 64

score_scale = 192.0 ** (-0.5)
route_scale = 2.5

Z_GROUPS = [[z * N_J + j for z in range(N_Z)] for j in range(N_J)]

VMEM = pl.BlockSpec(memory_space=pltpu.VMEM)
ANY = pl.BlockSpec(memory_space=pl.ANY)
SMEM = pl.BlockSpec(memory_space=pltpu.SMEM)


def along_y(value, step):
    pairs = [
        (a * N_Y + y, a * N_Y + (y + step) % N_Y) for a in range(2) for y in range(N_Y)
    ]
    return lax.ppermute(value, "section", pairs)


def across_x(value):
    pairs = [(s, (s + N_Y) % N_SECTION) for s in range(N_SECTION)]
    return lax.ppermute(value, "section", pairs)


def across_section(value, bits):
    return lax.ppermute(value, "section", [(s, s ^ bits) for s in range(N_SECTION)])


def across_j(value, bit):
    return lax.ppermute(value, "expert", [(e, e ^ bit) for e in range(N_EXPERT)])


def along_z(value, steps):
    return lax.ppermute(
        value, "expert", [(e, (e + steps * N_J) % N_EXPERT) for e in range(N_EXPERT)]
    )


def over_z(value):
    return lax.all_to_all(
        value, "expert", split_axis=0, concat_axis=0, tiled=True, axis_index_groups=Z_GROUPS
    )


def over_section(value):
    return lax.all_to_all(value, "section", split_axis=0, concat_axis=0, tiled=True)


def after(value, *others):
    return lax.optimization_barrier((value,) + others)[0]


def cost(flops, moved):
    return pl.CostEstimate(flops=flops, bytes_accessed=moved, transcendentals=0)


def params():
    return pltpu.CompilerParams(vmem_limit_bytes=60 * 1024 * 1024)


def prep_kernel(at_ref, unit_ref, tok_ref, ids_ref, aff_ref, cache_ref, out_ref):
    count, part = tok_ref.shape
    held, unit_len, qk = cache_ref.shape
    own_y, own_e = lax.rem(at_ref[0], N_Y), at_ref[1]
    affinity = aff_ref[...]
    high = affinity.astype(jnp.bfloat16).astype(jnp.float32)
    mid = (affinity - high).astype(jnp.bfloat16).astype(jnp.float32)
    low = affinity - high - mid
    names = jnp.concatenate([ids_ref[...].astype(jnp.float32), high, mid, low], 1)
    out_ref[0:count] = tok_ref[...]
    mine = jnp.int32(0)
    for i in range(unit_ref.shape[0]):
        unit = unit_ref[i]
        mine = mine + jnp.where(unit // held == own_e, unit % held, 0)
    extra = out_ref.shape[0] - count
    cut = unit_len // N_Y
    row = lax.broadcasted_iota(jnp.int32, (extra, unit_len), 0)
    column = lax.broadcasted_iota(jnp.int32, (extra, unit_len), 1)
    pick = jnp.where((column == own_y * cut + row) & (row < cut), 1.0, 0.0).astype(jnp.bfloat16)
    rows = jnp.dot(pick, cache_ref[mine], preferred_element_type=jnp.float32)
    names = jnp.concatenate([names, jnp.zeros((extra - 8, AUX), jnp.float32)], 0)
    rows = jnp.concatenate(
        [
            rows,
            jnp.zeros((extra, AUX_AT - qk), jnp.float32),
            names,
            jnp.zeros((extra, part - AUX_AT - AUX), jnp.float32),
        ],
        1,
    )
    out_ref[count:] = rows.astype(jnp.bfloat16)


def prep(at, unit_ids, tokens_b, expert_ids, affinity, cache_latent):
    count, width = tokens_b.shape
    part = width // N_SECTION
    rows = count + 16
    grid_spec = pltpu.PrefetchScalarGridSpec(
        num_scalar_prefetch=2,
        grid=(1,),
        in_specs=[
            pl.BlockSpec((count, part), lambda i, a, u: (0, a[0])),
            pl.BlockSpec((expert_ids.shape[1], count), lambda i, a, u: (0, 0)),
            pl.BlockSpec((expert_ids.shape[1], count), lambda i, a, u: (0, 0)),
            pl.BlockSpec(cache_latent.shape, lambda i, a, u: (0, 0, 0)),
        ],
        out_specs=pl.BlockSpec((rows, part), lambda i, a, u: (0, 0)),
    )
    return pl.pallas_call(
        prep_kernel,
        grid_spec=grid_spec,
        out_shape=jax.ShapeDtypeStruct((rows, part), jnp.bfloat16),
        compiler_params=params(),
        cost_estimate=cost(1000, 400 * 1024),
        name="prep",
    )(at, unit_ids, tokens_b, expert_ids.T, affinity.T, cache_latent)


def pack_kernel(e_ref, m_ref, c_ref, x_ref, xc_ref, slot_ref, share_ref, *out_refs):
    rows = N_Z * out_refs[0].shape[0]
    count = slot_ref.shape[1] // N_J
    refs = (m_ref, c_ref, x_ref, xc_ref)
    toks = jnp.concatenate([r[0:count, :] for r in refs], 0)
    total = toks.shape[0]
    aux = [r[count:, AUX_AT : AUX_AT + AUX].astype(jnp.float32)[0:8] for r in refs]
    ids, high, mid, low = [
        jnp.concatenate([a[:, k * count : (k + 1) * count] for a in aux], 1) for k in range(4)
    ]
    affinity = high + mid + low
    share = route_scale * affinity / jnp.sum(affinity, 0, keepdims=True)
    named, shares = [], []
    for step in range(N_Z):
        expert = lax.rem(e_ref[0] + step * N_J, N_EXPERT)
        hit = ids == expert.astype(jnp.float32)
        named.append(jnp.sum(jnp.where(hit, 1.0, 0.0), 0, keepdims=True))
        shares.append(jnp.sum(jnp.where(hit, share, 0.0), 0, keepdims=True))
    named = jnp.concatenate(named, 0)
    before = lax.broadcasted_iota(jnp.int32, (total, total), 0)
    later = lax.broadcasted_iota(jnp.int32, (total, total), 1)
    earlier = ((before // count) == (later // count)) & (before < later)
    rank = jnp.dot(
        named.astype(jnp.bfloat16),
        jnp.where(earlier, 1.0, 0.0).astype(jnp.bfloat16),
        preferred_element_type=jnp.float32,
    )
    source = lax.broadcasted_iota(jnp.int32, (N_Z, total), 1) // count
    slot = jnp.where(named > 0.5, rank + (source * CAP).astype(jnp.float32), -1.0)
    slot_ref[...] = slot
    share_ref[...] = jnp.concatenate(shares, 0)
    each = rows // N_Z
    place = lax.broadcasted_iota(jnp.int32, (N_Z, each, total), 1).astype(jnp.float32)
    pick = jnp.where(slot[:, None, :] == place, 1.0, 0.0).reshape(rows, total)
    got = jnp.dot(pick.astype(jnp.bfloat16), toks, preferred_element_type=jnp.float32)
    part = toks.shape[1]
    units = [r[count:, :AUX_AT].astype(jnp.float32)[0:8] for r in refs]
    rests = [u[:, LATENT : LATENT + REST] for u in units]
    rests = rests + [jnp.zeros((8, LATENT - N_J * REST), jnp.float32)]
    units = [u[:, :LATENT] for u in units] + [jnp.concatenate(rests, 1)]
    units = jnp.concatenate(units, 0)
    for step, out_ref in enumerate(out_refs):
        rows = jnp.concatenate([got[step * each : (step + 1) * each], units], 1)
        out_ref[...] = rows.astype(jnp.bfloat16)


def pack(own_e, messages, part):
    rows = N_J * CAP
    piece = jax.ShapeDtypeStruct((rows, part + LATENT), jnp.bfloat16)
    table = jax.ShapeDtypeStruct((N_Z, 128), jnp.float32)
    slot, share, *pieces = pl.pallas_call(
        pack_kernel,
        out_shape=(table,) * 2 + (piece,) * N_Z,
        in_specs=[SMEM] + [VMEM] * 4,
        out_specs=(VMEM,) * (2 + N_Z),
        compiler_params=params(),
        cost_estimate=cost(2 * N_Z * rows * 128 * part, 2 * N_Z * rows * part * 2),
        name="pack",
    )(own_e, *messages)
    return pieces, slot, share


def cut_kernel(in_ref, out_ref):
    part = out_ref.shape[2]
    for k in range(out_ref.shape[0]):
        out_ref[k] = in_ref[0, :, k * part : (k + 1) * part]


def cut_down(down_w):
    _, f, width = down_w.shape
    part = width // N_SECTION
    return pl.pallas_call(
        cut_kernel,
        out_shape=jax.ShapeDtypeStruct((N_SECTION, f, part), jnp.bfloat16),
        in_specs=[VMEM],
        out_specs=VMEM,
        compiler_params=params(),
        cost_estimate=cost(0, 2 * f * width * 2),
        name="cut_down",
    )(down_w)


def whole(shape):
    return pl.BlockSpec(shape, lambda i, s: (0,) * len(shape))


def sum_kernel(places, at_ref, *refs):
    xs, (gate, up, out_ref) = refs[:-3], refs[-3:]
    rows, part = xs[0].shape
    own_x, own_y = at_ref[0] // N_Y, lax.rem(at_ref[0], N_Y)
    total = None
    for b, (dx, dy) in enumerate(places):
        block = jnp.bitwise_xor(own_x, dx) * N_Y + lax.rem(own_y + dy, N_Y)
        k = pl.ds(pl.multiple_of(block * part, part), part)
        weights = jnp.concatenate([gate[0, k], up[0, k]], 1)
        x = jnp.concatenate([xs[2 * b][...], xs[2 * b + 1][...]], 0)
        term = jnp.dot(x, weights, preferred_element_type=jnp.float32)
        total = term if total is None else total + term
    f = out_ref.shape[2]
    gate, up = total[:, :f], total[:, f:]
    hidden = (gate / (1.0 + jnp.exp(-gate)) * up).astype(jnp.bfloat16)
    for s in range(out_ref.shape[0]):
        out_ref[s] = hidden


def add_blocks(at, blocks, gate_w, up_w):
    f = gate_w.shape[2]
    half, part = blocks[0][2][0].shape
    xs = [x for _, _, halves in blocks for x in halves]
    places = tuple((dx, dy) for dx, dy, _ in blocks)
    return pl.pallas_call(
        functools.partial(sum_kernel, places),
        out_shape=jax.ShapeDtypeStruct((N_SECTION, 2 * half, f), jnp.bfloat16),
        in_specs=[SMEM] + [VMEM] * (len(xs) + 2),
        out_specs=VMEM,
        compiler_params=params(),
        cost_estimate=cost(8 * half * part * f * len(blocks), 10 * 1024 * 1024),
        name="add_blocks",
    )(at, *xs, gate_w, up_w)


def down_kernel(e_ref, hid, w_ref, out_ref, h_buf, w_buf, h_sem, w_sem):
    count, _, f = hid.shape
    copies = []
    for k in range(count):
        at = pl.ds(k * f, f)
        mine = (
            pltpu.make_async_copy(hid.at[k], h_buf.at[:, at], h_sem.at[k]),
            pltpu.make_async_copy(w_ref.at[k], w_buf.at[at], w_sem.at[k]),
        )
        for copy in mine:
            copy.start()
        copies += mine
    for copy in copies:
        copy.wait()
    total = jnp.dot(h_buf[...], w_buf[...], preferred_element_type=jnp.float32)
    each = out_ref.shape[1]
    own_z = e_ref[0] // N_J
    for i, step in enumerate(Z_ORDER):
        rows = total[i * each : (i + 1) * each].astype(jnp.bfloat16)
        out_ref[lax.rem(own_z + N_Z - step, N_Z)] = rows


def down(own_e, hidden, weights):
    count, rows, f = hidden.shape
    part = weights.shape[2]
    return pl.pallas_call(
        down_kernel,
        out_shape=jax.ShapeDtypeStruct((N_Z, rows // N_Z, part), jnp.bfloat16),
        in_specs=[SMEM] + [ANY] * 2,
        out_specs=VMEM,
        scratch_shapes=[
            pltpu.VMEM((rows, count * f), jnp.bfloat16),
            pltpu.VMEM((count * f, part), jnp.bfloat16),
            pltpu.SemaphoreType.DMA((count,)),
            pltpu.SemaphoreType.DMA((count,)),
        ],
        compiler_params=params(),
        cost_estimate=cost(2 * rows * f * N_SECTION * part, 4 * 1024 * 1024),
        name="down",
    )(own_e, hidden, weights)


def units_kernel(e_ref, ids_ref, *refs):
    pieces, out_ref = refs[:-1], refs[-1]
    qk = out_ref.shape[1]
    rows = out_ref.shape[0] // ids_ref.shape[0]
    held = N_J * rows
    first = pieces[0].shape[1] - LATENT
    rest = qk - LATENT
    units = []
    for piece in pieces:
        rows_of = piece[:, first:].astype(jnp.float32)
        rests = [rows_of[held:, j * rest : (j + 1) * rest] for j in range(N_J)]
        units.append(jnp.concatenate([rows_of[:held], jnp.concatenate(rests, 0)], 1))
    units = jnp.concatenate(units, 0).astype(jnp.bfloat16)
    own_e = e_ref[0]
    row = lax.broadcasted_iota(jnp.int32, (rows, units.shape[0]), 0)
    column = lax.broadcasted_iota(jnp.int32, (rows, units.shape[0]), 1)
    picks = []
    for i in range(ids_ref.shape[0]):
        owner = ids_ref[i] // U_HELD
        step = lax.rem(own_e // N_J + N_Z - owner // N_J, N_Z)
        place = jnp.int32(0)
        for k, z_step in enumerate(Z_ORDER):
            place = place + jnp.where(step == z_step, k, 0)
        start = (place * N_J + lax.rem(jnp.bitwise_xor(owner, own_e), N_J)) * rows
        picks.append(jnp.where(column == row + start, 1.0, 0.0))
    picks = jnp.concatenate(picks, 0).astype(jnp.bfloat16)
    out_ref[...] = jnp.dot(picks, units, preferred_element_type=jnp.float32).astype(jnp.bfloat16)


def select_units(own_e, unit_ids, pieces, qk):
    return pl.pallas_call(
        units_kernel,
        out_shape=jax.ShapeDtypeStruct((unit_ids.shape[0] * 8, qk), jnp.bfloat16),
        in_specs=[SMEM, SMEM] + [VMEM] * len(pieces),
        out_specs=VMEM,
        compiler_params=params(),
        cost_estimate=cost(1000, 2 * 1024 * 1024),
        name="select_units",
    )(own_e, unit_ids, *pieces)


def mix_kernel(e_ref, slot_ref, share_ref, back_ref, own_ref, *out_refs):
    rows = back_ref.shape[0]
    own_z = e_ref[0] // N_J

    def by_z(ref):
        at = [lax.rem(z + N_Z - own_z, N_Z) for z in range(N_Z)]
        return jnp.concatenate([ref[pl.ds(k, 1), :] for k in at], 0)

    each = rows // N_Z
    total = slot_ref.shape[1]
    place = lax.broadcasted_iota(jnp.int32, (N_Z, each, total), 1).astype(jnp.float32)
    weight = jnp.where(by_z(slot_ref)[:, None, :] == place, by_z(share_ref)[:, None, :], 0.0)
    weight = weight.reshape(rows, total)
    high = weight.astype(jnp.bfloat16)
    low = (weight - high.astype(jnp.float32)).astype(jnp.bfloat16)
    back = back_ref[...]
    dims = (((0,), (0,)), ((), ()))
    got = lax.dot_general(high, back, dims, preferred_element_type=jnp.float32)
    got = got + lax.dot_general(low, back, dims, preferred_element_type=jnp.float32)
    count = own_ref.shape[0]
    own_ref[...] = got[:count]
    for p, out_ref in enumerate(out_refs, 1):
        out_ref[...] = got[p * count : (p + 1) * count].astype(jnp.bfloat16)


def mix(own_e, slot, share, back):
    rows, part = back.shape
    count = slot.shape[1] // N_J
    return pl.pallas_call(
        mix_kernel,
        out_shape=(jax.ShapeDtypeStruct((count, part), jnp.float32),)
        + (jax.ShapeDtypeStruct((count, part), jnp.bfloat16),) * (N_J - 1),
        in_specs=[SMEM] + [VMEM] * 3,
        out_specs=(VMEM,) * N_J,
        compiler_params=params(),
        cost_estimate=cost(4 * rows * N_J * count * part, rows * part * 4),
        name="mix",
    )(own_e, slot, share, back)


def attend_kernel(first_step, s_ref, q_ref, prev_ref, own_ref, *refs):
    unit_refs, (out_ref, keys_ref, units_ref) = refs[:N_Y], refs[-3:]
    block, heads = BLOCK, q_ref.shape[0] // BLOCK
    count = own_ref.shape[0]
    step = pl.program_id(0) + first_step

    @pl.when(step == first_step)
    def _():
        keys_ref[0:count] = prev_ref[...]
        keys_ref[count:] = own_ref[...]
        for i, unit_ref in enumerate(unit_refs):
            rows = unit_ref.shape[0]
            units_ref[i * rows : (i + 1) * rows] = unit_ref[...]

    span = count + block
    keys = keys_ref[pl.ds(pl.multiple_of(step * block, block), span), :]
    units = units_ref[...]
    q = q_ref[...]
    dims = (((1,), (1,)), ((), ()))
    win = lax.dot_general(q, keys, dims, preferred_element_type=jnp.float32) * score_scale
    far = lax.dot_general(q, units, dims, preferred_element_type=jnp.float32) * score_scale
    token = lax.broadcasted_iota(jnp.int32, win.shape, 0) // heads
    key = lax.broadcasted_iota(jnp.int32, win.shape, 1)
    first = jnp.where(s_ref[0] == 0, count - step * block, 0)
    allowed = (key > token) & (key <= token + count) & (key >= first)
    win = jnp.where(allowed, win, -1e30)
    top = jnp.maximum(jnp.max(win, 1, keepdims=True), jnp.max(far, 1, keepdims=True))
    win = jnp.exp(win - top)
    far = jnp.exp(far - top)
    denominator = jnp.sum(win, 1, keepdims=True) + jnp.sum(far, 1, keepdims=True)
    got = jnp.dot(win.astype(jnp.bfloat16), keys[:, :LATENT], preferred_element_type=jnp.float32)
    got = got + jnp.dot(
        far.astype(jnp.bfloat16), units[:, :LATENT], preferred_element_type=jnp.float32
    )
    out_ref[...] = (got / denominator).astype(jnp.bfloat16)


def attend(own_e, queries, previous, group_latent, unit_rows, first_step, steps, context=None):
    count, qk = group_latent.shape
    heads = queries.shape[0] // count
    rows = BLOCK * heads
    operands = [queries, previous, group_latent, *unit_rows]
    specs = [pl.BlockSpec((rows, qk), lambda i, s: (i + first_step, 0))]
    specs += [whole(x.shape) for x in operands[1:]]
    aliases = {}
    if context is not None:
        aliases = {1 + len(operands): 0}
        operands.append(context)
        specs.append(pl.BlockSpec(memory_space=pl.ANY))
    return pl.pallas_call(
        functools.partial(attend_kernel, first_step),
        grid_spec=pltpu.PrefetchScalarGridSpec(
            num_scalar_prefetch=1,
            grid=(steps,),
            in_specs=specs,
            out_specs=pl.BlockSpec((rows, LATENT), lambda i, s: (i + first_step, 0)),
            scratch_shapes=[
                pltpu.VMEM((2 * count, qk), jnp.bfloat16),
                pltpu.VMEM((N_Y * unit_rows[0].shape[0], qk), jnp.bfloat16),
            ],
        ),
        out_shape=jax.ShapeDtypeStruct((count * heads, LATENT), jnp.bfloat16),
        input_output_aliases=aliases,
        compiler_params=params(),
        cost_estimate=cost(1000 * 1000 * 1000 * steps, 2 * 1024 * 1024 * steps),
        name="attend",
    )(own_e, *operands)


def per_device(
    queries,
    group_latent,
    cache_latent,
    unit_ids,
    tokens_b,
    expert_ids,
    affinity,
    gate_w,
    up_w,
    down_w,
):
    own_s = lax.axis_index("section")
    own_e = lax.axis_index("expert")
    at = jnp.stack([own_s, own_e]).astype(jnp.int32)
    tok_count, width = tokens_b.shape
    part = width // N_SECTION
    qk = cache_latent.shape[2]

    message = prep(at, unit_ids, tokens_b, expert_ids, affinity, cache_latent)
    messages = (message,) + tuple(across_j(message, bit) for bit in (1, 2, 3))
    previous = lax.ppermute(
        group_latent, "expert", [(i, i + 1) for i in range(N_EXPERT - 1)]
    )

    down_cut = cut_down(after(down_w, message))
    down_all = over_section(after(down_cut, *messages))

    own_e = own_e[None].astype(jnp.int32)
    pieces, slot, share = pack(own_e, messages, part)
    pieces = [along_z(pieces[step], step) if step else pieces[step] for step in Z_ORDER]
    first, second = (
        jnp.concatenate([piece[:, :part] for piece in pieces[i : i + 4]], 0) for i in (0, 4)
    )
    second = after(second, down_all)

    before_1 = along_y(first, 1)
    after_2 = along_y(second, -1)
    x_1 = across_x(first)
    before_2 = along_y(second, 1)
    after_1 = along_y(first, -1)
    x_2 = across_x(second)
    far_1 = along_y(before_1, 1)
    far_2 = along_y(after_2, -1)
    before_x = [along_y(x_1, 1), along_y(x_2, 1)]
    after_x = [along_y(x_1, -1), along_y(x_2, -1)]

    far_x = [across_x(far_1), across_x(far_2)]
    blocks = [
        (0, 0, [first, second]),
        (0, 3, [before_1, before_2]),
        (0, 1, [after_1, after_2]),
        (1, 0, [x_1, x_2]),
        (0, 2, [far_1, far_2]),
        (1, 3, before_x),
        (1, 1, after_x),
        (1, 2, far_x),
    ]
    hidden = over_section(add_blocks(at, blocks, gate_w, up_w))

    units = select_units(own_e, unit_ids, pieces, qk)
    hidden, rows_q, units = lax.optimization_barrier(
        (hidden, queries.reshape(-1, qk), units)
    )
    unit_rows = (units, along_y(units, 1), along_y(units, -1), along_y(units, 2))
    back = over_z(down(own_e, hidden, down_all)).reshape(-1, part)

    keys = (previous, group_latent, unit_rows)
    steps = group_latent.shape[0] // BLOCK
    back, *_ = lax.optimization_barrier((back, unit_rows))
    context = attend(at[1:], after(rows_q, back), *keys, 0, 1)
    kept, *passed = mix(own_e, slot, share, back)
    passed = [across_j(value, bit) for bit, value in enumerate(passed, 1)]
    passed, context = lax.optimization_barrier((passed, context))
    out_part = kept + sum(value.astype(jnp.float32) for value in passed)
    out_part = out_part.astype(jnp.bfloat16)
    out_part = jnp.broadcast_to(out_part[None], (N_SECTION, tok_count, part))
    context = attend(at[1:], after(rows_q, *passed), *keys, 1, steps - 1, context)
    context = context.reshape(queries.shape[0], queries.shape[1], LATENT)
    moe_out = over_section(out_part).transpose(1, 0, 2).reshape(tok_count, width)
    return (context, moe_out)


def solution(mesh):
    return jax.shard_map(
        per_device,
        mesh=mesh,
        in_specs=(
            P("expert", "section", None),
            P("expert", None),
            P("expert", None, None),
            P(),
            P("expert", None),
            P("expert", None),
            P("expert", None),
            P("expert", None, "section"),
            P("expert", None, "section"),
            P("expert", "section", None),
        ),
        out_specs=(P("expert", "section", None), P("expert", None)),
        check_vma=False,
    )
```
